32 devices in a mesh: dp: 8 (over z, y), head: 4 (over x, core).
Axes of the slice: x: 2, y: 2, z: 4, core: 2. Of those that a mesh axis runs over, the one named last changes fastest.
Arguments:
- queries: bfloat16 [8192, 4096], P('dp', 'head'), may hold values from -6 to 6
- keys: bfloat16 [8192, 4096], P('dp', 'head'), may hold values from -6 to 6
- values: bfloat16 [8192, 4096], P('dp', 'head'), may hold values from -100 to 100
- out_grad: bfloat16 [8192, 4096], P('dp', 'head'), may hold values from -6 to 6
- norm_gain: float32 [4096], P('head'), may hold values from 0.1 to 1.9
- decay_table: float32 [16, 8], P('head'), may hold values from 0 to 0.52, as said below
- decay_index: int32 [16, 8192], P('head', 'dp'), may hold values from 0 to 7
- rollout_lengths: int32 [6], replicated, may hold values from 1 to 4096, 8192 in all
- move_partner: int32 [8], replicated, may hold values from 0 to 7, as said below
- move_slot: int32 [8], replicated, may hold values from 0 to 31, as said below
Outputs:
- query_grad: bfloat16 [8192, 4096], P('dp', 'head')
- key_grad: bfloat16 [8192, 4096], P('dp', 'head')
- value_grad: bfloat16 [8192, 4096], P('dp', 'head')
The draws below stay inside these ranges and needn't reach their ends.
Inputs may be any that keep to these rules, and one draw needn't show every extreme that they name: `decay_table`: positive rates. `rollout_lengths`: they sum to 8192. move_partner[d] is either d itself or a row whose index differs from d in exactly one bit, and the partner of the partner is the row itself. `move_slot`: one block of each row.
All inputs are finite; a program needn't handle non-finite values.
Results may differ from the reference program's by a relative error of at most 0.0063.
Values may be sent and summed in bfloat16 or wider, within the bound.
A program may use at most 128 MiB of HBM per device.

```python
import math
import jax
import jax.numpy as jnp
import numpy as np
from jax import lax

HEAD_DIM = 256
RETENTION_HEADS = 16
DECAY_LEVELS = 8
BLOCK_LEN = 32
ROW_BLOCKS = 32
ROLLOUTS = 6
ROW_TOKENS = 1024
DATA_ROWS = 8
TOKEN_TOTAL = 8192
FEATURES = 4096


def draw_values(key, part):
    first_key = jax.random.fold_in(key, 0)
    head_of = (jnp.arange(FEATURES) // HEAD_DIM).astype(jnp.float32)
    column_scale = 10.0 ** (head_of / (RETENTION_HEADS - 1))
    base = jnp.clip(jax.random.normal(first_key, (TOKEN_TOTAL, FEATURES), jnp.float32), -6.0, 6.0)
    return (base * column_scale[None, :]).astype(jnp.bfloat16)


def draw_decay_table(key, part):
    permute_random_key, gradual_random_key, quick_random_key, spike_random_key = jax.random.split(key, 4)
    order = jax.random.permutation(permute_random_key, RETENTION_HEADS)
    fast_count = RETENTION_HEADS // 2
    is_fast = order < fast_count
    slow_base = jax.random.uniform(gradual_random_key, (RETENTION_HEADS,), jnp.float32, 0.1, 0.5) * math.log(10.0) / TOKEN_TOTAL
    fast_base = 1.0 / jax.random.uniform(quick_random_key, (RETENTION_HEADS,), jnp.float32, 30.0, 50.0)
    base_rate = jnp.where(is_fast, fast_base, slow_base)
    factors = jnp.array([0.5, 0.8, 1.25, 2.0], jnp.float32)
    steady_level = base_rate[:, None] * factors[None, :]
    loss_values = jax.random.uniform(spike_random_key, (RETENTION_HEADS, DECAY_LEVELS - 4), jnp.float32, 0.2, 0.4)
    spike_flags = -jnp.log(1.0 - loss_values)
    return jnp.concatenate([steady_level, spike_flags], axis=1).astype(jnp.float32)


def draw_decay_index(key, part):
    block_random_key, spike_random_key, level_random_key = jax.random.split(key, 3)
    spans = (TOKEN_TOTAL + 255) // 256
    steady_level = jax.random.randint(block_random_key, (RETENTION_HEADS, spans), 0, 4)
    steady_level = jnp.repeat(steady_level, 256, axis=1)[:, :TOKEN_TOTAL]
    is_spiking = jax.random.randint(spike_random_key, (RETENTION_HEADS, TOKEN_TOTAL), 0, 8192) == 0
    spike_level = jax.random.randint(level_random_key, (RETENTION_HEADS, TOKEN_TOTAL), 4, DECAY_LEVELS)
    return jnp.where(is_spiking, spike_level, steady_level).astype(jnp.int32)


def draw_move_partner(key, part):
    levels = DATA_ROWS.bit_length() - 1
    level_keys = jax.random.split(key, levels + 1)
    row_ids = jnp.arange(DATA_ROWS, dtype=jnp.int32)
    partner = row_ids
    for level in reversed(range(levels)):
        other = jnp.bitwise_xor(row_ids, 1 << level).astype(jnp.int32)
        flags = jax.random.randint(level_keys[level], (DATA_ROWS,), 0, 2)
        lower = jnp.minimum(row_ids, other)
        wanted = flags[lower] == 1
        unpaired = (partner == row_ids) & (partner[other] == other)
        partner = jnp.where(wanted & unpaired, other, partner).astype(jnp.int32)
    chosen = (jax.random.randint(level_keys[levels], (), 0, DATA_ROWS // 2) * 2).astype(jnp.int32)
    first_old = partner[chosen]
    second_old = partner[chosen + 1]
    partner = partner.at[first_old].set(first_old).at[second_old].set(second_old)
    partner = partner.at[chosen].set(chosen + 1).at[chosen + 1].set(chosen)
    return partner.astype(jnp.int32)


def draw_move_slot(key, part):
    slot_key, pick_key = jax.random.split(key, 2)
    slots = jax.random.randint(slot_key, (DATA_ROWS,), 0, ROW_BLOCKS)
    chosen = jax.random.randint(pick_key, (), 0, DATA_ROWS)
    return jnp.where(jnp.arange(DATA_ROWS) == chosen, ROW_BLOCKS - 1, slots).astype(jnp.int32)


def block_scale(rng, shape, cuts, low, high):
    def one(dim, blocks):
        steps = jax.random.uniform(jax.random.fold_in(jax.random.fold_in(rng, 6), dim), (blocks,), jnp.float32, low / len(cuts), high / len(cuts))
        return jnp.repeat(jnp.exp(steps), shape[dim] // blocks).reshape((-1,) + (1,) * (len(shape) - dim - 1))

    factor_of = one(*cuts[0])
    for cut in cuts[1:]:
        factor_of = factor_of * one(*cut)
    return factor_of


def split_up(count, total, most, skew):
    portions = [(1 << 20) // math.isqrt(standing ** skew) + 1 for standing in range(2, count + 1)]
    rest, holding = total - most - (count - 1), [1] * (count - 1)
    while rest > 0:
        free = [i for i in range(count - 1) if holding[i] < most]
        pool, left = sum([portions[i] for i in free]), rest
        for i in free:
            addition = min(most - holding[i], max(1, left * portions[i] // pool), rest)
            holding[i] = holding[i] + addition
            rest = rest - addition
    return np.array([most] + holding)


def uneven(rng, number_of, total, most, lean):
    if number_of == 2:
        one = jax.random.randint(rng, (), max(1, total - most), min(most, total - 1) + 1)
        return jnp.stack([one, total - one])
    tallies = jnp.asarray(split_up(number_of, total, most, lean), jnp.int32)
    couples = (number_of - 1) // 2
    giver, taker = tallies[1:1 + 2 * couples:2], tallies[2:2 + 2 * couples:2]
    margin = jnp.minimum(giver - 1, most - taker)
    passed = jax.random.randint(jax.random.fold_in(rng, 1), (couples,), 0, 1 << 20) % (margin + 1)
    tallies = tallies.at[1:1 + 2 * couples:2].set(giver - passed).at[2:2 + 2 * couples:2].set(taker + passed)
    return tallies[jax.random.permutation(jax.random.fold_in(rng, 2), number_of)]


def gaussian(stream_key, extent, spread, reach, pieces=(), kind=jnp.bfloat16):
    result = jax.random.normal(stream_key, extent, jnp.float32) * spread
    if len(pieces) > 0:
        result = block_scale(stream_key, extent, pieces, -0.22, 0.18) * result
    return jnp.clip(result, min=-reach, max=reach).astype(kind)


def setup_inputs(seed: int = 0) -> dict:
    key_of = jax.random.split(jax.random.key(seed), 11)
    queries = gaussian(key_of[0], (TOKEN_TOTAL, FEATURES), 1.0, 6.0, ((0, 8), (1, 4)))
    keys = gaussian(key_of[1], (TOKEN_TOTAL, FEATURES), 1.0, 6.0, ((0, 8), (1, 4)))
    values = draw_values(jax.random.fold_in(key_of[10], 71), 0)
    out_grad = gaussian(key_of[3], (TOKEN_TOTAL, FEATURES), 1.0, 6.0, ((0, 8), (1, 4)))
    norm_gain = jnp.clip(1.0 + 0.18 * jax.random.normal(key_of[4], (FEATURES,), jnp.float32), 0.1, 1.9)
    decay_table = draw_decay_table(jax.random.fold_in(key_of[10], 71), 0)
    decay_index = draw_decay_index(jax.random.fold_in(key_of[10], 71), 0)
    rollout_lengths = uneven(key_of[7], ROLLOUTS, TOKEN_TOTAL, TOKEN_TOTAL // 2, 2).astype(jnp.int32)
    move_partner = draw_move_partner(jax.random.fold_in(key_of[10], 71), 0)
    move_slot = draw_move_slot(jax.random.fold_in(key_of[10], 71), 0)
    return dict(queries=queries, keys=keys, values=values, out_grad=out_grad, norm_gain=norm_gain, decay_table=decay_table, decay_index=decay_index, rollout_lengths=rollout_lengths, move_partner=move_partner, move_slot=move_slot)


EPSILON = 1e-05
HIGHEST = lax.Precision.HIGHEST

def edge_factors(rate, flag):
    segment = jnp.cumsum(flag.astype(jnp.int32)).astype(jnp.int32)
    total = jnp.cumsum(rate, axis=1)
    first = jnp.where(segment[None, :] == 0, jnp.exp(-total), 0.0)
    last = jnp.where(segment[None, :] == segment[-1], jnp.exp(total - total[:, -1:]), 0.0)
    whole = jnp.where(segment[-1] == 0, jnp.exp(-total[:, -1]), 0.0)
    return (total, segment, first, last, whole)

def decay_matrix(total_row, segment):
    count = segment.shape[0]
    places = jnp.arange(count)
    inside = (segment[:, None] == segment[None, :]) & (places[:, None] >= places[None, :])
    return jnp.where(inside, jnp.exp(jnp.minimum(total_row[None, :] - total_row[:, None], 0.0)), 0.0)

def trade_blocks(stored, move_partner, move_slot):
    row_ids = jnp.arange(DATA_ROWS, dtype=jnp.int32)[:, None]
    block_ids = jnp.arange(ROW_BLOCKS, dtype=jnp.int32)[None, :]
    moved = block_ids == move_slot[:, None]
    source_row = jnp.where(moved, move_partner[:, None], row_ids).astype(jnp.int32)
    source_block = jnp.where(moved, move_slot[move_partner][:, None], block_ids).astype(jnp.int32)
    return stored[source_row, source_block]

def carry_step(state, item):
    local_row, whole = item
    return (whole[:, None, None] * state + local_row, state)

def round_half(array):
    return lax.optimization_barrier(array.astype(jnp.bfloat16)).astype(jnp.float32)

def reference(queries, keys, values, out_grad, norm_gain, decay_table, decay_index, rollout_lengths, move_partner, move_slot):

    def packed(array):
        shaped = array.reshape(DATA_ROWS, ROW_BLOCKS, BLOCK_LEN, FEATURES)
        return trade_blocks(shaped, move_partner, move_slot).reshape(DATA_ROWS, ROW_TOKENS, RETENTION_HEADS, HEAD_DIM)
    query_rows = packed(queries)
    key_rows = packed(keys)
    value_rows = packed(values)
    cotangent_rows = packed(out_grad).reshape(DATA_ROWS, ROW_TOKENS, FEATURES)
    index_stored = decay_index.T.reshape(DATA_ROWS, ROW_BLOCKS, BLOCK_LEN, RETENTION_HEADS)
    index_rows = trade_blocks(index_stored, move_partner, move_slot).reshape(DATA_ROWS, ROW_TOKENS, RETENTION_HEADS)
    level_ids = jnp.arange(DECAY_LEVELS, dtype=jnp.int32)
    rate_rows = lax.optimization_barrier(jnp.sum(jnp.where(index_rows[..., None] == level_ids, decay_table[None, None], 0.0), axis=-1))
    rate_rows = jnp.transpose(rate_rows, (0, 2, 1))
    starts = (jnp.cumsum(rollout_lengths) - rollout_lengths).astype(jnp.int32)
    position = jnp.arange(TOKEN_TOTAL, dtype=jnp.int32).reshape(DATA_ROWS, ROW_TOKENS)
    flag_rows = jnp.any(position[..., None] == starts, axis=-1)

    def local_state(inputs):
        key_row, value_row, rate, flag = inputs
        total, segment, first, last, whole = edge_factors(rate, flag)
        scaled = round_half(value_row.astype(jnp.float32) * last.T[:, :, None])
        state = jnp.einsum('shi,shj->hij', key_row.astype(jnp.float32), scaled, precision=HIGHEST)
        return (state, whole)
    local_states, wholes = lax.map(local_state, (key_rows, value_rows, rate_rows, flag_rows))
    zero_state = jnp.zeros((RETENTION_HEADS, HEAD_DIM, HEAD_DIM), jnp.float32)
    _, carry_in = lax.scan(carry_step, zero_state, (local_states, wholes))
    carry_in = round_half(carry_in)

    def forward_row(inputs):
        query_row, key_row, value_row, cotangent, rate, flag, state_in = inputs
        total, segment, first, last, whole = edge_factors(rate, flag)
        decay = jax.vmap(decay_matrix, (0, None))(total, segment)
        query_f = query_row.astype(jnp.float32)
        scores = jnp.einsum('thi,shi->hts', query_f, key_row.astype(jnp.float32), precision=HIGHEST)
        weights = (scores * decay / HEAD_DIM).astype(jnp.bfloat16)
        inner_part = jnp.einsum('hts,shj->thj', weights.astype(jnp.float32), value_row.astype(jnp.float32), precision=HIGHEST)
        cross_part = first.T[:, :, None] * jnp.einsum('thi,hij->thj', query_f, state_in, precision=HIGHEST) / HEAD_DIM
        retained = (inner_part + cross_part).reshape(ROW_TOKENS, FEATURES)
        scaled = norm_gain * cotangent.astype(jnp.float32)
        squares = lax.optimization_barrier(jnp.sum(retained * retained, axis=1))
        inner = lax.optimization_barrier(jnp.sum(scaled * retained, axis=1))
        recip = lax.rsqrt(squares / FEATURES + EPSILON)
        norm_grad = (recip[:, None] * scaled - (recip ** 3 * inner / FEATURES)[:, None] * retained).astype(jnp.bfloat16)
        grad_heads = norm_grad.reshape(ROW_TOKENS, RETENTION_HEADS, HEAD_DIM)
        weighted = round_half(grad_heads.astype(jnp.float32) * first.T[:, :, None])
        back_local = jnp.einsum('thi,thj->hij', query_f, weighted, precision=HIGHEST) / HEAD_DIM
        return (grad_heads, back_local)
    grad_rows, back_locals = lax.map(forward_row, (query_rows, key_rows, value_rows, cotangent_rows, rate_rows, flag_rows, carry_in))
    _, carry_back = lax.scan(carry_step, zero_state, (back_locals, wholes), reverse=True)
    carry_back = round_half(carry_back)

    def backward_row(inputs):
        query_row, key_row, value_row, grad_heads, rate, flag, state_in, state_back = inputs
        total, segment, first, last, whole = edge_factors(rate, flag)
        decay = jax.vmap(decay_matrix, (0, None))(total, segment)
        query_f = query_row.astype(jnp.float32)
        key_f = key_row.astype(jnp.float32)
        value_f = value_row.astype(jnp.float32)
        grad_f = grad_heads.astype(jnp.float32)
        scores = jnp.einsum('thi,shi->hts', query_f, key_f, precision=HIGHEST)
        weights = round_half(scores * decay / HEAD_DIM)
        grad_scores = jnp.einsum('thj,shj->hts', grad_f, value_f, precision=HIGHEST)
        grad_weights = round_half(grad_scores * decay / HEAD_DIM)
        query_part = jnp.einsum('hts,shi->thi', grad_weights, key_f, precision=HIGHEST)
        query_part = query_part + first.T[:, :, None] * jnp.einsum('thj,hij->thi', grad_f, state_in, precision=HIGHEST) / HEAD_DIM
        key_part = jnp.einsum('hts,thi->shi', grad_weights, query_f, precision=HIGHEST)
        key_part = key_part + last.T[:, :, None] * jnp.einsum('shj,hij->shi', value_f, state_back, precision=HIGHEST)
        value_part = jnp.einsum('hts,thj->shj', weights, grad_f, precision=HIGHEST)
        value_part = value_part + last.T[:, :, None] * jnp.einsum('shi,hij->shj', key_f, state_back, precision=HIGHEST)
        return (query_part.reshape(ROW_TOKENS, FEATURES).astype(jnp.bfloat16), key_part.reshape(ROW_TOKENS, FEATURES).astype(jnp.bfloat16), value_part.reshape(ROW_TOKENS, FEATURES).astype(jnp.bfloat16))
    query_back, key_back, value_back = lax.map(backward_row, (query_rows, key_rows, value_rows, grad_rows, rate_rows, flag_rows, carry_in, carry_back))

    def stored(array):
        shaped = array.reshape(DATA_ROWS, ROW_BLOCKS, BLOCK_LEN, FEATURES)
        return trade_blocks(shaped, move_partner, move_slot).reshape(TOKEN_TOTAL, FEATURES)
    return (stored(query_back), stored(key_back), stored(value_back))
```

```python
import functools

import jax
import jax.numpy as jnp
from jax import lax
from jax.experimental import pallas as pl
from jax.experimental.pallas import tpu as pltpu
from jax.sharding import PartitionSpec as P

HEAD_DIM = 256
BLOCK_LEN = 32
FEATURES = 4096
EPSILON = 1e-05
TILE = 256
MESH = pl.DeviceIdType.MESH
F32 = jnp.float32
BF16 = jnp.bfloat16


def dot_nt(a, b):
    return lax.dot_general(a, b, (((1,), (1,)), ((), ())), preferred_element_type=F32)


def dot_tn(a, b):
    return lax.dot_general(a, b, (((0,), (0,)), ((), ())), preferred_element_type=F32)


def dot_nn(a, b):
    return jnp.dot(a, b, preferred_element_type=F32)


def twice(col):
    return jnp.concatenate([col, col], axis=1)


def to_column(row, tokens):
    return jnp.transpose(jnp.broadcast_to(row, (128, tokens)))


def main_kernel(
    count, hcount, heads, tokens,
    lengths, partners, slots, table, index, gain, q_hbm, k_hbm, v_hbm, dy_hbm,
    dq_hbm, dk_hbm, dv_hbm, guest_out,
    pq, pk, pv, pdy, wts, decay, gw, ret, dkin, grad, colb, segc, cum_s,
    rate_out, rate_in, blk_out, blk_in, w_in, w_out,
    st_out, st_in, st_ret, carry, bk_in, bk_ret, cback,
    hs_out, hs_in, lv_out, lv_in,
    in_sem, out_sem, rate_ss, rate_rs, blk_ss, blk_rs, w_ss, w_rs,
    p1_ss, p1_rs, p2_ss, p2_rs, b1_ss, b1_rs, b2_ss, b2_rs, hs_ss, hs_rs, lv_ss, lv_rs,
):
    me = lax.axis_index("dp")
    hme = lax.axis_index("head")
    levels = count.bit_length() - 1
    length = BLOCK_LEN
    span = heads * HEAD_DIM // count
    tiles = tokens // TILE
    width = heads * HEAD_DIM
    inv = 1.0 / HEAD_DIM

    loads = []
    for i, (src, dst) in enumerate(((k_hbm, pk), (v_hbm, pv), (q_hbm, pq), (dy_hbm, pdy))):
        copy = pltpu.make_async_copy(src, dst, in_sem.at[i])
        copy.start()
        loads.append(copy)

    barrier = pltpu.get_barrier_semaphore()
    for o in range(1, count):
        pl.semaphore_signal(barrier, inc=1, device_id={"dp": lax.rem(me + o, count)}, device_id_type=MESH)
    for o in range(1, hcount):
        pl.semaphore_signal(barrier, inc=1, device_id={"head": lax.rem(hme + o, hcount)}, device_id_type=MESH)

    idx = index[...]
    rate = jnp.zeros((heads, tokens), F32)
    for level in range(table.shape[1]):
        rate = jnp.where(idx == level, table[:, level:level + 1], rate)
    rate_out[...] = jnp.zeros((8, tokens), F32)
    rate_out[0:heads, :] = rate

    slot = slots[me]
    partner = partners[me]
    partner_slot = slot
    for d in range(count):
        partner_slot = jnp.where(partner == d, slots[d], partner_slot)
    pl.semaphore_wait(barrier, count - 1 + hcount - 1)

    def remote(src, dst, ss, rs, axis, to):
        return pltpu.make_async_remote_copy(
            src_ref=src, dst_ref=dst, send_sem=ss, recv_sem=rs,
            device_id={axis: to}, device_id_type=MESH,
        )

    def other(level):
        bit = 1 << level
        return me + bit - 2 * bit * (lax.rem(me // bit, 2))

    rate_copies = []
    for level in range(levels):
        copy = remote(rate_out, rate_in.at[level], rate_ss.at[level], rate_rs.at[level], "dp", other(level))
        copy.start()
        rate_copies.append(copy)

    blocks = tokens // length

    def pick(ref):
        slot_of = jnp.full((length, width), slot, jnp.int32)

        def one(b, acc):
            part = ref[pl.ds(pl.multiple_of(b * length, length), length), :].astype(F32)
            return jnp.where(slot_of == b, part, acc)

        return lax.fori_loop(0, blocks, one, jnp.zeros((length, width), F32)).astype(BF16)

    for i, ref in enumerate((pk, pv, pq, pdy)):
        loads[i].wait()
        blk_out[i] = pick(ref)
    blk_copies = []
    for level in range(levels):
        copy = remote(blk_out, blk_in.at[level], blk_ss.at[level], blk_rs.at[level], "dp", other(level))
        copy.start()
        blk_copies.append(copy)

    lane = lax.broadcasted_iota(jnp.int32, (8, tokens), 1)
    sub = lax.broadcasted_iota(jnp.int32, (8, tokens), 0)
    flag = jnp.zeros((8, tokens), F32)
    start = jnp.int32(0)
    for n in range(lengths.shape[0]):
        flag = jnp.where(lane == start - me * tokens, 1.0, flag)
        start = start + lengths[n]

    own = rate_out[...]
    guest = own
    for level in range(levels):
        rate_copies[level].wait()
        guest = jnp.where(jnp.full((8, tokens), partner, jnp.int32) == other(level), rate_in[level], guest)
    shift = slot - partner_slot + blocks
    for bit in range(blocks.bit_length() - 1):
        here = (jnp.full((8, tokens), shift, jnp.int32) >> bit) & 1
        guest = jnp.where(here == 1, pltpu.roll(guest, length << bit, 1), guest)
    rows = jnp.where(lane // length == jnp.full((8, tokens), slot, jnp.int32), guest, own)
    cum = jnp.where(sub == heads, flag, rows)
    step = 1
    while step < tokens:
        cum = cum + jnp.where(lane >= step, pltpu.roll(cum, step, 1), 0.0)
        step *= 2
    cum_s[...] = cum
    seg = cum[heads:heads + 1, :]
    seg_last = cum[heads:heads + 1, tokens - 1:tokens]
    cum_last = cum[:, tokens - 1:tokens]
    first8 = jnp.where(seg == 0.0, jnp.exp(-cum), 0.0)
    last8 = jnp.where(seg == seg_last, jnp.exp(cum - cum_last), 0.0)
    whole8 = jnp.where(seg_last == 0.0, jnp.exp(-cum_last), 0.0)
    w_out[...] = jnp.broadcast_to(whole8, (8, 128))
    w_copies = []
    for o in range(1, count):
        to = lax.rem(me + o, count)
        copy = remote(w_out, w_in.at[me], w_ss.at[o], w_rs.at[me], "dp", to)
        copy.start()
        w_copies.append(copy)
    w_in[me] = w_out[...]
    for h in range(heads):
        colb[h] = to_column(cum[h:h + 1, :], tokens)
        colb[heads + h] = to_column(first8[h:h + 1, :], tokens)
        colb[2 * heads + h] = to_column(last8[h:h + 1, :], tokens)
    segc[...] = to_column(seg, tokens)

    def make_decay(h, _):
        for tb in range(tiles):
            base = tb * (tb + 1) // 2 * TILE
            trow = pl.ds(tb * TILE, TILE)
            ct = twice(colb[h, trow, :])
            sc = twice(segc[trow, :])
            for sb in range(tb + 1):
                scol = pl.ds(sb * TILE, TILE)
                inside = cum_s[heads:heads + 1, scol] == sc
                if sb == tb:
                    r = lax.broadcasted_iota(jnp.int32, (TILE, TILE), 0)
                    c = lax.broadcasted_iota(jnp.int32, (TILE, TILE), 1)
                    inside = inside & (r >= c)
                value = jnp.exp(jnp.minimum(cum_s[pl.ds(h, 1), scol] - ct, 0.0)) * inv
                decay[h, :, base + sb * TILE:base + (sb + 1) * TILE] = jnp.where(inside, value, 0.0)
        return 0

    lax.fori_loop(0, heads, make_decay, 0)

    for level in range(levels):
        blk_copies[level].wait()
    for i, ref in enumerate((pk, pv, pq, pdy)):
        block = blk_out[i].astype(F32)
        for level in range(levels):
            match = jnp.full(block.shape, partner, jnp.int32) == other(level)
            block = jnp.where(match, blk_in[level, i].astype(F32), block)

        def put(b, _, ref=ref, block=block):
            at = pl.ds(pl.multiple_of(b * length, length), length)
            here = jnp.full(block.shape, slot, jnp.int32) == b
            ref[at, :] = jnp.where(here, block, ref[at, :].astype(F32)).astype(BF16)
            return 0

        lax.fori_loop(0, blocks, put, 0)

    def columns(h):
        return pl.ds(pl.multiple_of(h * HEAD_DIM, HEAD_DIM), HEAD_DIM)

    def state_rows(h):
        return pl.ds(pl.multiple_of(h * HEAD_DIM, HEAD_DIM), HEAD_DIM)

    def span_rows(j):
        return pl.ds(pl.multiple_of(j * span, span), span)

    def scatter(inbox, ss, rs):
        copies = []
        for o in range(1, count):
            to = lax.rem(me + o, count)
            copy = remote(st_out.at[span_rows(to)], inbox.at[me], ss.at[o], rs.at[me], "dp", to)
            copy.start()
            copies.append(copy)
        inbox[me] = st_out[span_rows(me), :]
        return copies

    def prefix(inbox, rs, outbox, home, ss2, rs2, reverse):
        for o in range(1, count):
            frm = lax.rem(me + count - o, count)
            remote(st_out.at[span_rows(0)], inbox.at[frm], ss2.at[o], rs.at[frm], "dp", frm).wait_recv()
        head = me * span // HEAD_DIM

        def one(turn, run):
            d = count - 1 - turn if reverse else turn
            outbox[d] = run.astype(BF16)
            w = w_in[d, pl.ds(head, 1), :]
            return twice(w) * run + inbox[d].astype(F32)

        lax.fori_loop(0, count, one, jnp.zeros((span, HEAD_DIM), F32))
        copies = []
        for o in range(1, count):
            to = lax.rem(me + o, count)
            copy = remote(outbox.at[to], home.at[span_rows(me)], ss2.at[o], rs2.at[me], "dp", to)
            copy.start()
            copies.append(copy)
        home[span_rows(me), :] = outbox[me]
        return copies

    def gather_wait(home, outbox, ss2, rs2):
        for o in range(1, count):
            frm = lax.rem(me + count - o, count)
            remote(outbox.at[0], home.at[span_rows(frm)], ss2.at[o], rs2.at[frm], "dp", frm).wait_recv()

    def local_state(h, _):
        gated = (pv[:, columns(h)].astype(F32) * twice(colb[2 * heads + h])).astype(BF16)
        st_out[state_rows(h), :] = dot_tn(pk[:, columns(h)], gated).astype(BF16)
        return 0

    lax.fori_loop(0, heads, local_state, 0)
    p1 = scatter(st_in, p1_ss, p1_rs)

    def forward(h, _):
        cols = columns(h)
        for tb in range(tiles):
            n = (tb + 1) * TILE
            base = tb * (tb + 1) // 2 * TILE
            trow = pl.ds(tb * TILE, TILE)
            scores = dot_nt(pq[trow, cols], pk[0:n, cols])
            w = (scores * decay[h, :, base:base + n]).astype(BF16)
            wts[h, trow, 0:n] = w
            ret[trow, cols] = dot_nn(w, pv[0:n, cols])
        return 0

    half = heads // 2
    lax.fori_loop(0, half, forward, 0)
    for o in range(1, count):
        w_copies[o - 1].wait_send()
        frm = lax.rem(me + count - o, count)
        remote(w_out, w_in.at[frm], w_ss.at[o], w_rs.at[frm], "dp", frm).wait_recv()
    p2 = prefix(st_in, p1_rs, st_ret, carry, p2_ss, p2_rs, False)
    lax.fori_loop(half, heads, forward, 0)
    gather_wait(carry, st_ret, p2_ss, p2_rs)

    def cross(h, sums):
        cols = columns(h)
        part = dot_nn(pq[:, cols], carry[state_rows(h), :])
        r = ret[:, cols] + part * (twice(colb[heads + h]) * inv)
        ret[:, cols] = r
        s = gain[:, cols] * pdy[:, cols].astype(F32)
        sq = r * r
        sr = s * r
        return (sums[0] + sq[:, 0:128] + sq[:, 128:256], sums[1] + sr[:, 0:128] + sr[:, 128:256])

    zero = jnp.zeros((tokens, 128), F32)
    sums = lax.fori_loop(0, heads, cross, (zero, zero))
    sq_row = jnp.sum(jnp.transpose(sums[0]), axis=0, keepdims=True)
    in_row = jnp.sum(jnp.transpose(sums[1]), axis=0, keepdims=True)
    hs_out[...] = jnp.where(sub == 0, sq_row, in_row)
    h_copies = []
    for o in range(1, hcount):
        to = lax.rem(hme + o, hcount)
        copy = remote(hs_out, hs_in.at[hme], hs_ss.at[o], hs_rs.at[hme], "head", to)
        copy.start()
        h_copies.append(copy)
    both = hs_out[...]
    for o in range(1, hcount):
        frm = lax.rem(hme + hcount - o, hcount)
        remote(hs_out, hs_in.at[frm], hs_ss.at[o], hs_rs.at[frm], "head", frm).wait_recv()
        both = both + hs_in[frm]
    for copy in p1:
        copy.wait_send()
    recip = lax.rsqrt(both[0:1, :] * (1.0 / FEATURES) + EPSILON)
    coef = recip * recip * recip * both[1:2, :] * (1.0 / FEATURES)
    hs_cols = (to_column(recip, tokens), to_column(coef, tokens))
    segc[...] = hs_cols[0]
    dkin[:, 0:128] = hs_cols[1]

    def back_state(h, _):
        cols = columns(h)
        s = gain[:, cols] * pdy[:, cols].astype(F32)
        g = (twice(segc[...]) * s - twice(dkin[:, 0:128]) * ret[:, cols]).astype(BF16)
        grad[:, cols] = g
        gated = (g.astype(F32) * twice(colb[heads + h])).astype(BF16)
        st_out[state_rows(h), :] = (dot_tn(pq[:, cols], gated) * inv).astype(BF16)
        return 0

    lax.fori_loop(0, heads, back_state, 0)
    b1 = scatter(bk_in, b1_ss, b1_rs)

    def backward(h, _):
        cols = columns(h)
        for tb in range(tiles):
            n = (tb + 1) * TILE
            base = tb * (tb + 1) // 2 * TILE
            trow = pl.ds(tb * TILE, TILE)
            g = grad[trow, cols]
            scores = dot_nt(g, pv[0:n, cols])
            w = (scores * decay[h, :, base:base + n]).astype(BF16)
            gw[trow, 0:n] = w
            part = dot_nt(g, carry[state_rows(h), :])
            fc = twice(colb[heads + h, trow, :]) * inv
            pdy[trow, cols] = (dot_nn(w, pk[0:n, cols]) + fc * part).astype(BF16)
        for sb in range(tiles):
            lo = sb * TILE
            srow = pl.ds(lo, TILE)
            dkin[srow, cols] = dot_tn(gw[lo:, lo:lo + TILE], pq[lo:, cols])
            ret[srow, cols] = dot_tn(wts[h, lo:, lo:lo + TILE], grad[lo:, cols])
        return 0

    lax.fori_loop(0, half, backward, 0)
    b2 = prefix(bk_in, b1_rs, bk_ret, cback, b2_ss, b2_rs, True)
    lax.fori_loop(half, heads, backward, 0)
    gather_wait(cback, bk_ret, b2_ss, b2_rs)

    def finish(h, _):
        cols = columns(h)
        lc = twice(colb[2 * heads + h])
        state = cback[state_rows(h), :]
        k = pk[:, cols]
        dk = dkin[:, cols] + lc * dot_nt(pv[:, cols], state)
        dv = ret[:, cols] + lc * dot_nn(k, state)
        pk[:, cols] = dk.astype(BF16)
        pv[:, cols] = dv.astype(BF16)
        return 0

    lax.fori_loop(0, heads, finish, 0)
    for i, ref in enumerate((pdy, pk, pv)):
        lv_out[i] = pick(ref)
    lv_copies = []
    for level in range(levels):
        copy = remote(lv_out, lv_in.at[level], lv_ss.at[level], lv_rs.at[level], "dp", other(level))
        copy.start()
        lv_copies.append(copy)
    stores = []
    for i, (src, dst) in enumerate(((pdy, dq_hbm), (pk, dk_hbm), (pv, dv_hbm))):
        copy = pltpu.make_async_copy(src, dst, out_sem.at[i])
        copy.start()
        stores.append(copy)
    for copy in p2 + b1 + b2 + h_copies:
        copy.wait_send()
    for copy in lv_copies:
        copy.wait()
    for i in range(3):
        block = lv_out[i].astype(F32)
        for level in range(levels):
            match = jnp.full(block.shape, partner, jnp.int32) == other(level)
            block = jnp.where(match, lv_in[level, i].astype(F32), block)
        guest_out[i] = block.astype(BF16)
    for copy in stores:
        copy.wait()


def place_kernel(chunk, slot, guest, dq, dk, dv, oq, ok, ov):
    oq[...] = dq[...]
    ok[...] = dk[...]
    ov[...] = dv[...]
    first = pl.program_id(0) * chunk
    at = slot[0] * BLOCK_LEN - first

    @pl.when((at >= 0) & (at < chunk))
    def _():
        rows = pl.ds(pl.multiple_of(at, BLOCK_LEN), BLOCK_LEN)
        oq[rows, :] = guest[0]
        ok[rows, :] = guest[1]
        ov[rows, :] = guest[2]


def local(count, hcount, queries, keys, values, out_grad, norm_gain, table, index, lengths, partners, slots):
    tokens, width = queries.shape
    heads = table.shape[0]
    tiles = tokens // TILE
    levels = count.bit_length() - 1
    span = heads * HEAD_DIM // count
    smem = pl.BlockSpec(memory_space=pltpu.SMEM)
    vmem = pl.BlockSpec(memory_space=pltpu.VMEM)
    any_ = pl.BlockSpec(memory_space=pl.ANY)
    full = jax.ShapeDtypeStruct((tokens, width), BF16)
    V = pltpu.VMEM
    D = pltpu.SemaphoreType.DMA
    state = V((heads * HEAD_DIM, HEAD_DIM), BF16)
    part = V((count, span, HEAD_DIM), BF16)
    dq, dk, dv, guest = pl.pallas_call(
        functools.partial(main_kernel, count, hcount, heads, tokens),
        out_shape=(full, full, full, jax.ShapeDtypeStruct((3, BLOCK_LEN, width), BF16)),
        in_specs=[smem, smem, smem, vmem, vmem, vmem, any_, any_, any_, any_],
        out_specs=(any_, any_, any_, vmem),
        scratch_shapes=[
            V((tokens, width), BF16), V((tokens, width), BF16), V((tokens, width), BF16), V((tokens, width), BF16),
            V((heads, tokens, tokens), BF16),
            V((heads, TILE, tiles * (tiles + 1) // 2 * TILE), F32),
            V((tokens, tokens), BF16),
            V((tokens, width), F32), V((tokens, width), F32), V((tokens, width), BF16),
            V((3 * heads, tokens, 128), F32), V((tokens, 128), F32), V((8, tokens), F32),
            V((8, tokens), F32), V((levels, 8, tokens), F32),
            V((4, BLOCK_LEN, width), BF16), V((levels, 4, BLOCK_LEN, width), BF16),
            V((count, 8, 128), F32), V((8, 128), F32),
            state, part, part, state, part, part, state,
            V((8, tokens), F32), V((hcount, 8, tokens), F32),
            V((3, BLOCK_LEN, width), BF16), V((levels, 3, BLOCK_LEN, width), BF16),
            D((4,)), D((3,)), D((levels,)), D((levels,)), D((levels,)), D((levels,)),
            D((count,)), D((count,)), D((count,)), D((count,)), D((count,)), D((count,)),
            D((count,)), D((count,)), D((count,)), D((count,)),
            D((hcount,)), D((hcount,)), D((levels,)), D((levels,)),
        ],
        compiler_params=pltpu.CompilerParams(
            collective_id=0, has_side_effects=True, vmem_limit_bytes=60 * 1024 * 1024
        ),
    )(lengths, partners, slots, table, index, norm_gain.reshape(1, width), queries, keys, values, out_grad)

    slot = lax.dynamic_slice_in_dim(slots, lax.axis_index("dp"), 1, 0)
    chunk = 256
    block = pl.BlockSpec((chunk, width), lambda i: (i, 0))
    return pl.pallas_call(
        functools.partial(place_kernel, chunk),
        grid=(tokens // chunk,),
        out_shape=(full, full, full),
        in_specs=[smem, pl.BlockSpec((3, BLOCK_LEN, width), lambda i: (0, 0, 0)), block, block, block],
        out_specs=(block, block, block),
    )(slot, guest, dq, dk, dv)


def solution(mesh):
    placed = (
        P("dp", "head"), P("dp", "head"), P("dp", "head"), P("dp", "head"),
        P("head"), P("head", None), P("head", "dp"), P(), P(), P(),
    )
    return jax.shard_map(
        functools.partial(local, mesh.shape["dp"], mesh.shape["head"]),
        mesh=mesh,
        in_specs=placed,
        out_specs=(P("dp", "head"), P("dp", "head"), P("dp", "head")),
        check_vma=False,
    )
```

```python
import functools

import jax
import jax.numpy as jnp
from jax import lax
from jax.experimental import pallas as pl
from jax.experimental.pallas import tpu as pltpu
from jax.sharding import PartitionSpec as P

HEAD_DIM = 256
BLOCK_LEN = 32
FEATURES = 4096
EPSILON = 1e-05
TILE = 256
MESH = pl.DeviceIdType.MESH
F32 = jnp.float32
BF16 = jnp.bfloat16


def dot_nt(a, b):
    return lax.dot_general(a, b, (((1,), (1,)), ((), ())), preferred_element_type=F32)


def dot_tn(a, b):
    return lax.dot_general(a, b, (((0,), (0,)), ((), ())), preferred_element_type=F32)


def dot_nn(a, b):
    return jnp.dot(a, b, preferred_element_type=F32)


def twice(col):
    return jnp.concatenate([col, col], axis=1)


def to_column(row, tokens):
    return jnp.transpose(jnp.broadcast_to(row, (128, tokens)))


def main_kernel(
    count, hcount, heads, tokens,
    lengths, partners, slots, table, index, gain, q_hbm, k_hbm, v_hbm, dy_hbm,
    dq_hbm, dk_hbm, dv_hbm, guest_out,
    pq, pk, pv, pdy, wts, decay, gw, ret, dkin, grad, colb, segc, cum_s,
    sel, unsel, rate_out, rate_in, blk_out, blk_in, w_in, w_out,
    st_out, st_in, st_ret, carry, bk_in, bk_ret, cback, mid_out, mid_in,
    hs_out, hs_in, lv_out, lv_in,
    in_sem, out_sem, rate_ss, rate_rs, blk_ss, blk_rs, w_ss, w_rs,
    p1_ss, p1_rs, p2_ss, p2_rs, b1_ss, b1_rs, b2_ss, b2_rs, mid_ss, mid_rs, hs_ss, hs_rs, lv_ss, lv_rs,
):
    me = lax.axis_index("dp")
    hme = lax.axis_index("head")
    levels = count.bit_length() - 1
    length = BLOCK_LEN
    group = count // 2
    side = me // group
    base_row = side * group
    pos = me - base_row
    mate = me + group - 2 * group * side
    span = heads * HEAD_DIM // group
    tiles = tokens // TILE
    width = heads * HEAD_DIM
    inv = 1.0 / HEAD_DIM

    loads = []
    for i, (src, dst) in enumerate(((k_hbm, pk), (v_hbm, pv), (q_hbm, pq), (dy_hbm, pdy))):
        copy = pltpu.make_async_copy(src, dst, in_sem.at[i])
        copy.start()
        loads.append(copy)

    barrier = pltpu.get_barrier_semaphore()
    for o in range(1, count):
        pl.semaphore_signal(barrier, inc=1, device_id={"dp": lax.rem(me + o, count)}, device_id_type=MESH)
    for o in range(1, hcount):
        pl.semaphore_signal(barrier, inc=1, device_id={"head": lax.rem(hme + o, hcount)}, device_id_type=MESH)

    idx = index[...]
    rate = jnp.zeros((heads, tokens), F32)
    for level in range(table.shape[1]):
        rate = jnp.where(idx == level, table[:, level:level + 1], rate)
    rate_out[...] = jnp.zeros((8, tokens), F32)
    rate_out[0:heads, :] = rate

    slot = slots[me]
    partner = partners[me]
    partner_slot = slot
    for d in range(count):
        partner_slot = jnp.where(partner == d, slots[d], partner_slot)
    pl.semaphore_wait(barrier, count - 1 + hcount - 1)

    def remote(src, dst, ss, rs, axis, to):
        return pltpu.make_async_remote_copy(
            src_ref=src, dst_ref=dst, send_sem=ss, recv_sem=rs,
            device_id={axis: to}, device_id_type=MESH,
        )

    def other(level):
        bit = 1 << level
        return me + bit - 2 * bit * (lax.rem(me // bit, 2))

    rate_copies = []
    for level in range(levels):
        copy = remote(rate_out, rate_in.at[level], rate_ss.at[level], rate_rs.at[level], "dp", other(level))
        copy.start()
        rate_copies.append(copy)

    blocks = tokens // length

    chosen = lax.broadcasted_iota(jnp.int32, (tokens, 128), 0) // length == jnp.full((tokens, 128), slot, jnp.int32)
    sel[...] = jnp.where(chosen, 1.0, 0.0).astype(BF16)
    unsel[...] = jnp.where(chosen, 0.0, 1.0).astype(BF16)

    def widen(mask):
        return jnp.concatenate([mask] * (width // 128), axis=1)

    def pick(ref):
        def one(b, acc):
            at = pl.ds(pl.multiple_of(b * length, length), length)
            return acc + ref[at, :] * widen(sel[at, :])

        return lax.fori_loop(0, blocks, one, jnp.zeros((length, width), BF16))

    def to_partners(out, inbox, ss, rs, first):
        copies = []
        for level in range(levels):
            copy = remote(out, inbox(level), ss.at[first + level], rs.at[first + level], "dp", other(level))
            copy.start()
            copies.append(copy)
        return copies

    def guest_of(own_block, inbox):
        block = own_block.astype(F32)
        for level in range(levels):
            match = jnp.full(block.shape, partner, jnp.int32) == other(level)
            block = jnp.where(match, inbox(level).astype(F32), block)
        return block.astype(BF16)

    def put(ref, i):
        block = guest_of(blk_out[i], lambda level: blk_in[level, i])

        def one(b, _):
            at = pl.ds(pl.multiple_of(b * length, length), length)
            ref[at, :] = ref[at, :] * widen(unsel[at, :]) + block * widen(sel[at, :])
            return 0

        lax.fori_loop(0, blocks, one, 0)

    packed = (pk, pv, pq, pdy)

    def load_and_pick(i):
        loads[i].wait()
        blk_out[i] = pick(packed[i])

    load_and_pick(0)
    load_and_pick(1)
    kv_copies = to_partners(blk_out.at[0:2], lambda level: blk_in.at[level, 0:2], blk_ss, blk_rs, 0)
    load_and_pick(2)
    q_copies = to_partners(blk_out.at[2], lambda level: blk_in.at[level, 2], blk_ss, blk_rs, levels)
    load_and_pick(3)

    lane = lax.broadcasted_iota(jnp.int32, (8, tokens), 1)
    sub = lax.broadcasted_iota(jnp.int32, (8, tokens), 0)
    flag = jnp.zeros((8, tokens), F32)
    start = jnp.int32(0)
    for n in range(lengths.shape[0]):
        flag = jnp.where(lane == start - me * tokens, 1.0, flag)
        start = start + lengths[n]

    own = rate_out[...]
    guest = own
    for level in range(levels):
        rate_copies[level].wait()
        guest = jnp.where(jnp.full((8, tokens), partner, jnp.int32) == other(level), rate_in[level], guest)
    shift = slot - partner_slot + blocks
    for bit in range(blocks.bit_length() - 1):
        here = (jnp.full((8, tokens), shift, jnp.int32) >> bit) & 1
        guest = jnp.where(here == 1, pltpu.roll(guest, length << bit, 1), guest)
    rows = jnp.where(lane // length == jnp.full((8, tokens), slot, jnp.int32), guest, own)
    cum = jnp.where(sub == heads, flag, rows)
    step = 1
    while step < tokens:
        cum = cum + jnp.where(lane >= step, pltpu.roll(cum, step, 1), 0.0)
        step *= 2
    cum_s[...] = cum
    seg = cum[heads:heads + 1, :]
    seg_last = cum[heads:heads + 1, tokens - 1:tokens]
    cum_last = cum[:, tokens - 1:tokens]
    first8 = jnp.where(seg == 0.0, jnp.exp(-cum), 0.0)
    last8 = jnp.where(seg == seg_last, jnp.exp(cum - cum_last), 0.0)
    whole8 = jnp.where(seg_last == 0.0, jnp.exp(-cum_last), 0.0)
    w_out[...] = jnp.broadcast_to(whole8, (8, 128))
    w_copies = []
    for o in range(1, count):
        to = lax.rem(me + o, count)
        copy = remote(w_out, w_in.at[me], w_ss.at[o], w_rs.at[me], "dp", to)
        copy.start()
        w_copies.append(copy)
    w_in[me] = w_out[...]
    for h in range(heads):
        colb[h] = to_column(cum[h:h + 1, :], tokens)
        colb[heads + h] = to_column(first8[h:h + 1, :], tokens)
        colb[2 * heads + h] = to_column(last8[h:h + 1, :], tokens)
    segc[...] = to_column(seg, tokens)

    def make_decay(h, _):
        for tb in range(tiles):
            base = tb * (tb + 1) // 2 * TILE
            trow = pl.ds(tb * TILE, TILE)
            ct = twice(colb[h, trow, :])
            sc = twice(segc[trow, :])
            for sb in range(tb + 1):
                scol = pl.ds(sb * TILE, TILE)
                inside = cum_s[heads:heads + 1, scol] == sc
                if sb == tb:
                    r = lax.broadcasted_iota(jnp.int32, (TILE, TILE), 0)
                    c = lax.broadcasted_iota(jnp.int32, (TILE, TILE), 1)
                    inside = inside & (r >= c)
                value = jnp.exp(jnp.minimum(cum_s[pl.ds(h, 1), scol] - ct, 0.0)) * inv
                decay[h, :, base + sb * TILE:base + (sb + 1) * TILE] = jnp.where(inside, value, 0.0)
        return 0

    lax.fori_loop(0, heads, make_decay, 0)

    for copy in kv_copies:
        copy.wait()
    put(pk, 0)
    put(pv, 1)

    def columns(h):
        return pl.ds(pl.multiple_of(h * HEAD_DIM, HEAD_DIM), HEAD_DIM)

    def state_rows(h):
        return pl.ds(pl.multiple_of(h * HEAD_DIM, HEAD_DIM), HEAD_DIM)

    def span_rows(j):
        return pl.ds(pl.multiple_of(j * span, span), span)

    def scatter(inbox, ss, rs):
        copies = []
        for o in range(1, group):
            to = lax.rem(pos + o, group)
            copy = remote(st_out.at[span_rows(to)], inbox.at[pos], ss.at[o], rs.at[pos], "dp", base_row + to)
            copy.start()
            copies.append(copy)
        inbox[pos] = st_out[span_rows(pos), :]
        return copies

    head_of_span = pos * span // HEAD_DIM

    def fold(inbox, run, reverse, outbox):
        def one(turn, run):
            d = group - 1 - turn if reverse else turn
            if outbox is not None:
                outbox[d] = run.astype(BF16)
            w = w_in[base_row + d, pl.ds(head_of_span, 1), :]
            return twice(w) * run + inbox[d].astype(F32)

        return lax.fori_loop(0, group, one, run)

    def across(inbox, rs, ss, which, reverse):
        for o in range(1, group):
            frm = lax.rem(pos + group - o, group)
            remote(st_out.at[span_rows(0)], inbox.at[frm], ss.at[o], rs.at[frm], "dp", base_row + frm).wait_recv()
        mid_out[which] = fold(inbox, jnp.zeros((span, HEAD_DIM), F32), reverse, None).astype(BF16)
        copy = remote(mid_out.at[which], mid_in.at[which], mid_ss.at[which], mid_rs.at[which], "dp", mate)
        copy.start()
        return copy

    def prefix(inbox, outbox, home, ss2, rs2, which, copy, reverse):
        copy.wait_recv()
        behind = jnp.full((span, HEAD_DIM), side, jnp.int32) == (0 if reverse else 1)
        run = jnp.where(behind, mid_in[which].astype(F32), 0.0)
        fold(inbox, run, reverse, outbox)
        copies = []
        for o in range(1, group):
            to = lax.rem(pos + o, group)
            out = remote(outbox.at[to], home.at[span_rows(pos)], ss2.at[o], rs2.at[pos], "dp", base_row + to)
            out.start()
            copies.append(out)
        home[span_rows(pos), :] = outbox[pos]
        return copies

    def gather_wait(home, outbox, ss2, rs2):
        for o in range(1, group):
            frm = lax.rem(pos + group - o, group)
            remote(outbox.at[0], home.at[span_rows(frm)], ss2.at[o], rs2.at[frm], "dp", base_row + frm).wait_recv()

    def local_state(h, _):
        gated = (pv[:, columns(h)].astype(F32) * twice(colb[2 * heads + h])).astype(BF16)
        st_out[state_rows(h), :] = dot_tn(pk[:, columns(h)], gated).astype(BF16)
        return 0

    lax.fori_loop(0, heads, local_state, 0)
    p1 = scatter(st_in, p1_ss, p1_rs)
    dy_copies = to_partners(blk_out.at[3], lambda level: blk_in.at[level, 3], blk_ss, blk_rs, 2 * levels)
    for copy in q_copies:
        copy.wait()
    put(pq, 2)

    def forward(h, _):
        cols = columns(h)
        for tb in range(tiles):
            n = (tb + 1) * TILE
            base = tb * (tb + 1) // 2 * TILE
            trow = pl.ds(tb * TILE, TILE)
            scores = dot_nt(pq[trow, cols], pk[0:n, cols])
            w = (scores * decay[h, :, base:base + n]).astype(BF16)
            wts[h, trow, 0:n] = w
            ret[trow, cols] = dot_nn(w, pv[0:n, cols])
        return 0

    cut_a, cut_b = heads // 2, 3 * heads // 4
    lax.fori_loop(0, cut_a, forward, 0)
    for o in range(1, count):
        w_copies[o - 1].wait_send()
        frm = lax.rem(me + count - o, count)
        remote(w_out, w_in.at[frm], w_ss.at[o], w_rs.at[frm], "dp", frm).wait_recv()
    mid = across(st_in, p1_rs, p1_ss, 0, False)
    lax.fori_loop(cut_a, cut_b, forward, 0)
    p2 = prefix(st_in, st_ret, carry, p2_ss, p2_rs, 0, mid, False)
    lax.fori_loop(cut_b, heads, forward, 0)
    for copy in dy_copies:
        copy.wait()
    put(pdy, 3)
    gather_wait(carry, st_ret, p2_ss, p2_rs)

    def cross(h, sums):
        cols = columns(h)
        part = dot_nn(pq[:, cols], carry[state_rows(h), :])
        r = ret[:, cols] + part * (twice(colb[heads + h]) * inv)
        ret[:, cols] = r
        s = gain[:, cols] * pdy[:, cols].astype(F32)
        sq = r * r
        sr = s * r
        return (sums[0] + sq[:, 0:128] + sq[:, 128:256], sums[1] + sr[:, 0:128] + sr[:, 128:256])

    zero = jnp.zeros((tokens, 128), F32)
    sums = lax.fori_loop(0, heads, cross, (zero, zero))
    sq_row = jnp.sum(jnp.transpose(sums[0]), axis=0, keepdims=True)
    in_row = jnp.sum(jnp.transpose(sums[1]), axis=0, keepdims=True)
    hs_out[...] = jnp.where(sub == 0, sq_row, in_row)
    h_copies = []
    for o in range(1, hcount):
        to = lax.rem(hme + o, hcount)
        copy = remote(hs_out, hs_in.at[hme], hs_ss.at[o], hs_rs.at[hme], "head", to)
        copy.start()
        h_copies.append(copy)
    both = hs_out[...]
    for o in range(1, hcount):
        frm = lax.rem(hme + hcount - o, hcount)
        remote(hs_out, hs_in.at[frm], hs_ss.at[o], hs_rs.at[frm], "head", frm).wait_recv()
        both = both + hs_in[frm]
    for copy in p1:
        copy.wait_send()
    recip = lax.rsqrt(both[0:1, :] * (1.0 / FEATURES) + EPSILON)
    coef = recip * recip * recip * both[1:2, :] * (1.0 / FEATURES)
    hs_cols = (to_column(recip, tokens), to_column(coef, tokens))
    segc[...] = hs_cols[0]
    dkin[:, 0:128] = hs_cols[1]

    def back_state(h, _):
        cols = columns(h)
        s = gain[:, cols] * pdy[:, cols].astype(F32)
        g = (twice(segc[...]) * s - twice(dkin[:, 0:128]) * ret[:, cols]).astype(BF16)
        grad[:, cols] = g
        gated = (g.astype(F32) * twice(colb[heads + h])).astype(BF16)
        st_out[state_rows(h), :] = (dot_tn(pq[:, cols], gated) * inv).astype(BF16)
        return 0

    lax.fori_loop(0, heads, back_state, 0)
    b1 = scatter(bk_in, b1_ss, b1_rs)

    def backward(h, _):
        cols = columns(h)
        for tb in range(tiles):
            n = (tb + 1) * TILE
            base = tb * (tb + 1) // 2 * TILE
            trow = pl.ds(tb * TILE, TILE)
            g = grad[trow, cols]
            scores = dot_nt(g, pv[0:n, cols])
            w = (scores * decay[h, :, base:base + n]).astype(BF16)
            gw[trow, 0:n] = w
            part = dot_nt(g, carry[state_rows(h), :])
            fc = twice(colb[heads + h, trow, :]) * inv
            pdy[trow, cols] = (dot_nn(w, pk[0:n, cols]) + fc * part).astype(BF16)
        for sb in range(tiles):
            lo = sb * TILE
            srow = pl.ds(lo, TILE)
            dkin[srow, cols] = dot_tn(gw[lo:, lo:lo + TILE], pq[lo:, cols])
            ret[srow, cols] = dot_tn(wts[h, lo:, lo:lo + TILE], grad[lo:, cols])
        return 0

    lax.fori_loop(0, cut_a, backward, 0)
    back_mid = across(bk_in, b1_rs, b1_ss, 1, True)
    lax.fori_loop(cut_a, cut_b, backward, 0)
    b2 = prefix(bk_in, bk_ret, cback, b2_ss, b2_rs, 1, back_mid, True)
    lax.fori_loop(cut_b, heads, backward, 0)
    lv_out[0] = pick(pdy)
    lv_copies = to_partners(lv_out.at[0], lambda level: lv_in.at[level, 0], lv_ss, lv_rs, 0)
    stores = [pltpu.make_async_copy(pdy, dq_hbm, out_sem.at[0])]
    stores[0].start()
    gather_wait(cback, bk_ret, b2_ss, b2_rs)

    def finish(h, _):
        cols = columns(h)
        lc = twice(colb[2 * heads + h])
        state = cback[state_rows(h), :]
        k = pk[:, cols]
        dk = dkin[:, cols] + lc * dot_nt(pv[:, cols], state)
        dv = ret[:, cols] + lc * dot_nn(k, state)
        pk[:, cols] = dk.astype(BF16)
        pv[:, cols] = dv.astype(BF16)
        return 0

    lax.fori_loop(0, heads, finish, 0)
    lv_out[1] = pick(pk)
    lv_out[2] = pick(pv)
    lv_copies += to_partners(lv_out.at[1:3], lambda level: lv_in.at[level, 1:3], lv_ss, lv_rs, levels)
    for i, (src, dst) in enumerate(((pk, dk_hbm), (pv, dv_hbm))):
        copy = pltpu.make_async_copy(src, dst, out_sem.at[i + 1])
        copy.start()
        stores.append(copy)
    for copy in p2 + b1 + b2 + h_copies + [mid, back_mid]:
        copy.wait_send()
    for copy in lv_copies:
        copy.wait()
    for i in range(3):
        guest_out[i] = guest_of(lv_out[i], lambda level: lv_in[level, i])
    for copy in stores:
        copy.wait()


def place_kernel(chunk, slots, guest, dq, dk, dv, oq, ok, ov):
    oq[...] = dq[...]
    ok[...] = dk[...]
    ov[...] = dv[...]
    first = pl.program_id(0) * chunk
    at = slots[lax.axis_index("dp")] * BLOCK_LEN - first

    @pl.when((at >= 0) & (at < chunk))
    def _():
        rows = pl.ds(pl.multiple_of(at, BLOCK_LEN), BLOCK_LEN)
        oq[rows, :] = guest[0]
        ok[rows, :] = guest[1]
        ov[rows, :] = guest[2]


def local(count, hcount, queries, keys, values, out_grad, norm_gain, table, index, lengths, partners, slots):
    tokens, width = queries.shape
    heads = table.shape[0]
    tiles = tokens // TILE
    levels = count.bit_length() - 1
    group = count // 2
    span = heads * HEAD_DIM // group
    smem = pl.BlockSpec(memory_space=pltpu.SMEM)
    vmem = pl.BlockSpec(memory_space=pltpu.VMEM)
    any_ = pl.BlockSpec(memory_space=pl.ANY)
    full = jax.ShapeDtypeStruct((tokens, width), BF16)
    V = pltpu.VMEM
    D = pltpu.SemaphoreType.DMA
    state = V((heads * HEAD_DIM, HEAD_DIM), BF16)
    part = V((group, span, HEAD_DIM), BF16)
    dq, dk, dv, guest = pl.pallas_call(
        functools.partial(main_kernel, count, hcount, heads, tokens),
        out_shape=(full, full, full, jax.ShapeDtypeStruct((3, BLOCK_LEN, width), BF16)),
        in_specs=[smem, smem, smem, vmem, vmem, vmem, any_, any_, any_, any_],
        out_specs=(any_, any_, any_, vmem),
        scratch_shapes=[
            V((tokens, width), BF16), V((tokens, width), BF16), V((tokens, width), BF16), V((tokens, width), BF16),
            V((heads, tokens, tokens), BF16),
            V((heads, TILE, tiles * (tiles + 1) // 2 * TILE), F32),
            V((tokens, tokens), BF16),
            V((tokens, width), F32), V((tokens, width), F32), V((tokens, width), BF16),
            V((3 * heads, tokens, 128), F32), V((tokens, 128), F32), V((8, tokens), F32),
            V((tokens, 128), BF16), V((tokens, 128), BF16),
            V((8, tokens), F32), V((levels, 8, tokens), F32),
            V((4, BLOCK_LEN, width), BF16), V((levels, 4, BLOCK_LEN, width), BF16),
            V((count, 8, 128), F32), V((8, 128), F32),
            state, part, part, state, part, part, state,
            V((2, span, HEAD_DIM), BF16), V((2, span, HEAD_DIM), BF16),
            V((8, tokens), F32), V((hcount, 8, tokens), F32),
            V((3, BLOCK_LEN, width), BF16), V((levels, 3, BLOCK_LEN, width), BF16),
            D((4,)), D((3,)), D((levels,)), D((levels,)), D((3 * levels,)), D((3 * levels,)),
            D((count,)), D((count,)), D((group,)), D((group,)), D((group,)), D((group,)),
            D((group,)), D((group,)), D((group,)), D((group,)), D((2,)), D((2,)),
            D((hcount,)), D((hcount,)), D((2 * levels,)), D((2 * levels,)),
        ],
        compiler_params=pltpu.CompilerParams(
            collective_id=0, has_side_effects=True, vmem_limit_bytes=60 * 1024 * 1024
        ),
    )(lengths, partners, slots, table, index, norm_gain.reshape(1, width), queries, keys, values, out_grad)

    chunk = 128
    block = pl.BlockSpec((chunk, width), lambda i: (i, 0))
    return pl.pallas_call(
        functools.partial(place_kernel, chunk),
        grid=(tokens // chunk,),
        out_shape=(full, full, full),
        in_specs=[smem, pl.BlockSpec((3, BLOCK_LEN, width), lambda i: (0, 0, 0)), block, block, block],
        out_specs=(block, block, block),
    )(slots, guest, dq, dk, dv)


def solution(mesh):
    placed = (
        P("dp", "head"), P("dp", "head"), P("dp", "head"), P("dp", "head"),
        P("head"), P("head", None), P("head", "dp"), P(), P(), P(),
    )
    return jax.shard_map(
        functools.partial(local, mesh.shape["dp"], mesh.shape["head"]),
        mesh=mesh,
        in_specs=placed,
        out_specs=(P("dp", "head"), P("dp", "head"), P("dp", "head")),
        check_vma=False,
    )
```

```python
import functools

import jax
import jax.numpy as jnp
from jax import lax
from jax.experimental import pallas as pl
from jax.experimental.pallas import tpu as pltpu
from jax.sharding import PartitionSpec as P

HEAD_DIM = 256
BLOCK_LEN = 32
FEATURES = 4096
EPSILON = 1e-05
TILE = 256
MESH = pl.DeviceIdType.MESH
F32 = jnp.float32
BF16 = jnp.bfloat16


def dot_nt(a, b):
    return lax.dot_general(a, b, (((1,), (1,)), ((), ())), preferred_element_type=F32)


def dot_tn(a, b):
    return lax.dot_general(a, b, (((0,), (0,)), ((), ())), preferred_element_type=F32)


def dot_nn(a, b):
    return jnp.dot(a, b, preferred_element_type=F32)


def twice(col):
    return jnp.concatenate([col, col], axis=1)


def to_column(row, tokens):
    return jnp.transpose(jnp.broadcast_to(row, (128, tokens)))


def main_kernel(
    count, hcount, heads, tokens,
    lengths, partners, slots, table, index, gain, q_hbm, k_hbm, v_hbm, dy_hbm,
    pdy, pk, pv, guest_out,
    pq, wts, decay, gw, ret, dkin, grad, colb, segc, cum_s,
    sel, unsel, guest_kv, last_g, fin, rate_out, rate_in, blk_out, blk_in, w_in, w_out,
    st_out, st_in, st_ret, carry, bk_in, bk_ret, cback, mid_out, mid_in,
    hs_out, hs_in, lv_out, lv_in,
    in_sem, rate_ss, rate_rs, blk_ss, blk_rs, w_ss, w_rs,
    p1_ss, p1_rs, p2_ss, p2_rs, b1_ss, b1_rs, b2_ss, b2_rs, mid_ss, mid_rs, hs_ss, hs_rs, lv_ss, lv_rs,
):
    me = lax.axis_index("dp")
    hme = lax.axis_index("head")
    levels = count.bit_length() - 1
    length = BLOCK_LEN
    group = count // 2
    side = me // group
    base_row = side * group
    pos = me - base_row
    mate = me + group - 2 * group * side
    span = heads * HEAD_DIM // group
    sub_span = span // 2
    tiles = tokens // TILE
    width = heads * HEAD_DIM
    inv = 1.0 / HEAD_DIM

    loads = []
    for i, (src, dst) in enumerate(((k_hbm, pk), (v_hbm, pv), (q_hbm, pq), (dy_hbm, pdy))):
        copy = pltpu.make_async_copy(src, dst, in_sem.at[i])
        copy.start()
        loads.append(copy)

    barrier = pltpu.get_barrier_semaphore()
    for o in range(1, count):
        pl.semaphore_signal(barrier, inc=1, device_id={"dp": lax.rem(me + o, count)}, device_id_type=MESH)
    for o in range(1, hcount):
        pl.semaphore_signal(barrier, inc=1, device_id={"head": lax.rem(hme + o, hcount)}, device_id_type=MESH)

    idx = index[...]
    rate = jnp.zeros((heads, tokens), F32)
    for level in range(table.shape[1]):
        rate = jnp.where(idx == level, table[:, level:level + 1], rate)
    rate_out[...] = jnp.zeros((8, tokens), F32)
    rate_out[0:heads, :] = rate

    slot = slots[me]
    partner = partners[me]
    partner_slot = slot
    for d in range(count):
        partner_slot = jnp.where(partner == d, slots[d], partner_slot)
    pl.semaphore_wait(barrier, count - 1 + hcount - 1)

    def remote(src, dst, ss, rs, axis, to):
        return pltpu.make_async_remote_copy(
            src_ref=src, dst_ref=dst, send_sem=ss, recv_sem=rs,
            device_id={axis: to}, device_id_type=MESH,
        )

    def other(level):
        bit = 1 << level
        return me + bit - 2 * bit * (lax.rem(me // bit, 2))

    rate_copies = []
    for level in range(levels):
        copy = remote(rate_out, rate_in.at[level], rate_ss.at[level], rate_rs.at[level], "dp", other(level))
        copy.start()
        rate_copies.append(copy)

    blocks = tokens // length

    chosen = lax.broadcasted_iota(jnp.int32, (tokens, 128), 0) // length == jnp.full((tokens, 128), slot, jnp.int32)
    sel[...] = jnp.where(chosen, 1.0, 0.0).astype(BF16)
    unsel[...] = jnp.where(chosen, 0.0, 1.0).astype(BF16)

    def widen(mask):
        return jnp.concatenate([mask] * (width // 128), axis=1)

    def pick(ref):
        def one(b, acc):
            at = pl.ds(pl.multiple_of(b * length, length), length)
            return acc + ref[at, :] * widen(sel[at, :])

        return lax.fori_loop(0, blocks, one, jnp.zeros((length, width), BF16))

    def to_partners(out, inbox, ss, rs, first):
        copies = []
        for level in range(levels):
            copy = remote(out, inbox(level), ss.at[first + level], rs.at[first + level], "dp", other(level))
            copy.start()
            copies.append(copy)
        return copies

    def guest_of(own_block, inbox):
        block = own_block.astype(F32)
        for level in range(levels):
            match = jnp.full(block.shape, partner, jnp.int32) == other(level)
            block = jnp.where(match, inbox(level).astype(F32), block)
        return block.astype(BF16)

    def put(ref, block):
        def one(b, _):
            at = pl.ds(pl.multiple_of(b * length, length), length)
            ref[at, :] = ref[at, :] * widen(unsel[at, :]) + block * widen(sel[at, :])
            return 0

        lax.fori_loop(0, blocks, one, 0)

    packed = (pk, pv, pq, pdy)

    def load_and_pick(i):
        loads[i].wait()
        blk_out[i] = pick(packed[i])

    load_and_pick(0)
    load_and_pick(1)
    kv_copies = to_partners(blk_out.at[0:2], lambda level: blk_in.at[level, 0:2], blk_ss, blk_rs, 0)
    load_and_pick(2)
    q_copies = to_partners(blk_out.at[2], lambda level: blk_in.at[level, 2], blk_ss, blk_rs, levels)
    load_and_pick(3)

    lane = lax.broadcasted_iota(jnp.int32, (8, tokens), 1)
    sub = lax.broadcasted_iota(jnp.int32, (8, tokens), 0)
    flag = jnp.zeros((8, tokens), F32)
    start = jnp.int32(0)
    for n in range(lengths.shape[0]):
        flag = jnp.where(lane == start - me * tokens, 1.0, flag)
        start = start + lengths[n]

    own = rate_out[...]
    guest = own
    for level in range(levels):
        rate_copies[level].wait()
        guest = jnp.where(jnp.full((8, tokens), partner, jnp.int32) == other(level), rate_in[level], guest)
    shift = slot - partner_slot + blocks
    for bit in range(blocks.bit_length() - 1):
        here = (jnp.full((8, tokens), shift, jnp.int32) >> bit) & 1
        guest = jnp.where(here == 1, pltpu.roll(guest, length << bit, 1), guest)
    rows = jnp.where(lane // length == jnp.full((8, tokens), slot, jnp.int32), guest, own)
    cum = jnp.where(sub == heads, flag, rows)
    step = 1
    while step < tokens:
        cum = cum + jnp.where(lane >= step, pltpu.roll(cum, step, 1), 0.0)
        step *= 2
    cum_s[...] = cum
    seg = cum[heads:heads + 1, :]
    seg_last = cum[heads:heads + 1, tokens - 1:tokens]
    cum_last = cum[:, tokens - 1:tokens]
    first8 = jnp.where(seg == 0.0, jnp.exp(-cum), 0.0)
    last8 = jnp.where(seg == seg_last, jnp.exp(cum - cum_last), 0.0)
    whole8 = jnp.where(seg_last == 0.0, jnp.exp(-cum_last), 0.0)
    w_out[...] = jnp.broadcast_to(whole8, (8, 128))
    w_copies = []
    for o in range(1, count):
        to = lax.rem(me + o, count)
        copy = remote(w_out, w_in.at[me], w_ss.at[o], w_rs.at[me], "dp", to)
        copy.start()
        w_copies.append(copy)
    w_in[me] = w_out[...]
    for h in range(heads):
        colb[h] = to_column(cum[h:h + 1, :], tokens)
        colb[heads + h] = to_column(first8[h:h + 1, :], tokens)
        colb[2 * heads + h] = to_column(last8[h:h + 1, :], tokens)
    segc[...] = to_column(seg, tokens)

    def columns(h):
        return pl.ds(pl.multiple_of(h * HEAD_DIM, HEAD_DIM), HEAD_DIM)

    def state_rows(h):
        return pl.ds(pl.multiple_of(h * HEAD_DIM, HEAD_DIM), HEAD_DIM)

    def span_rows(j):
        return pl.ds(pl.multiple_of(j * span, span), span)

    def part_rows(j, c):
        return pl.ds(pl.multiple_of(j * span + c * sub_span, sub_span), sub_span)

    def half_rows(c):
        return pl.ds(c * sub_span, sub_span)

    def scatter(inbox, ss, rs, c):
        copies = []
        for o in range(1, group):
            to = lax.rem(pos + o, group)
            copy = remote(
                st_out.at[part_rows(to, c)], inbox.at[pos, half_rows(c)],
                ss.at[c * group + o], rs.at[c * group + pos], "dp", base_row + to,
            )
            copy.start()
            copies.append(copy)
        inbox[pos, half_rows(c), :] = st_out[part_rows(pos, c), :]
        return copies

    head_of_span = pos * span // HEAD_DIM

    def fold(inbox, run, reverse, outbox, c):
        def one(turn, run):
            d = group - 1 - turn if reverse else turn
            if outbox is not None:
                outbox[d, half_rows(c), :] = run.astype(BF16)
            w = w_in[base_row + d, pl.ds(head_of_span, 1), :]
            return twice(w) * run + inbox[d, half_rows(c), :].astype(F32)

        return lax.fori_loop(0, group, one, run)

    def across(inbox, rs, ss, which, reverse, c):
        for o in range(1, group):
            frm = lax.rem(pos + group - o, group)
            remote(
                st_out.at[part_rows(0, c)], inbox.at[frm, half_rows(c)],
                ss.at[c * group + o], rs.at[c * group + frm], "dp", base_row + frm,
            ).wait_recv()
        at = 2 * which + c
        mid_out[at] = fold(inbox, jnp.zeros((sub_span, HEAD_DIM), F32), reverse, None, c).astype(BF16)
        copy = remote(mid_out.at[at], mid_in.at[at], mid_ss.at[at], mid_rs.at[at], "dp", mate)
        copy.start()
        return copy

    def prefix(inbox, outbox, home, ss2, rs2, which, copy, reverse, c):
        copy.wait_recv()
        behind = jnp.full((sub_span, HEAD_DIM), side, jnp.int32) == (0 if reverse else 1)
        run = jnp.where(behind, mid_in[2 * which + c].astype(F32), 0.0)
        fold(inbox, run, reverse, outbox, c)
        copies = []
        for o in range(1, group):
            to = lax.rem(pos + o, group)
            out = remote(
                outbox.at[to, half_rows(c)], home.at[part_rows(pos, c)],
                ss2.at[c * group + o], rs2.at[c * group + pos], "dp", base_row + to,
            )
            out.start()
            copies.append(out)
        home[part_rows(pos, c), :] = outbox[pos, half_rows(c), :]
        return copies

    def gather_wait(home, outbox, ss2, rs2):
        for c in range(2):
            for o in range(1, group):
                frm = lax.rem(pos + group - o, group)
                remote(
                    outbox.at[0, half_rows(c)], home.at[part_rows(frm, c)],
                    ss2.at[c * group + o], rs2.at[c * group + frm], "dp", base_row + frm,
                ).wait_recv()

    def kept_state(h, _):
        last = colb[2 * heads + h]
        gated = (pv[:, columns(h)].astype(F32) * twice(last)).astype(BF16) * twice(unsel[...])
        dkin[state_rows(h), 0:HEAD_DIM] = dot_tn(pk[:, columns(h)], gated)

        def one(b, acc):
            at = pl.ds(pl.multiple_of(b * length, length), length)
            return acc + colb[2 * heads + h, at, :] * sel[at, :].astype(F32)

        last_g[h] = lax.fori_loop(0, blocks, one, jnp.zeros((length, 128), F32))
        return 0

    lax.fori_loop(0, heads, kept_state, 0)

    def make_decay(h, _):
        for tb in range(tiles):
            base = tb * (tb + 1) // 2 * TILE
            trow = pl.ds(tb * TILE, TILE)
            ct = twice(colb[h, trow, :])
            sc = twice(segc[trow, :])
            for sb in range(tb + 1):
                scol = pl.ds(sb * TILE, TILE)
                inside = cum_s[heads:heads + 1, scol] == sc
                if sb == tb:
                    r = lax.broadcasted_iota(jnp.int32, (TILE, TILE), 0)
                    c = lax.broadcasted_iota(jnp.int32, (TILE, TILE), 1)
                    inside = inside & (r >= c)
                value = jnp.exp(jnp.minimum(cum_s[pl.ds(h, 1), scol] - ct, 0.0)) * inv
                decay[h, :, base + sb * TILE:base + (sb + 1) * TILE] = jnp.where(inside, value, 0.0)
        return 0

    lax.fori_loop(0, heads, make_decay, 0)

    for copy in kv_copies:
        copy.wait()
    for i in range(2):
        guest_kv[i] = guest_of(blk_out[i], lambda level: blk_in[level, i])

    def local_state(h, _):
        gated = (guest_kv[1, :, columns(h)].astype(F32) * twice(last_g[h])).astype(BF16)
        state = dkin[state_rows(h), 0:HEAD_DIM] + dot_tn(guest_kv[0, :, columns(h)], gated)
        st_out[state_rows(h), :] = state.astype(BF16)
        return 0

    lax.fori_loop(0, heads, local_state, 0)
    p1 = scatter(st_in, p1_ss, p1_rs, 0) + scatter(st_in, p1_ss, p1_rs, 1)
    dy_copies = to_partners(blk_out.at[3], lambda level: blk_in.at[level, 3], blk_ss, blk_rs, 2 * levels)
    put(pk, guest_kv[0])
    put(pv, guest_kv[1])
    for copy in q_copies:
        copy.wait()
    put(pq, guest_of(blk_out[2], lambda level: blk_in[level, 2]))

    def forward(h, _):
        cols = columns(h)
        for tb in range(tiles):
            n = (tb + 1) * TILE
            base = tb * (tb + 1) // 2 * TILE
            trow = pl.ds(tb * TILE, TILE)
            scores = dot_nt(pq[trow, cols], pk[0:n, cols])
            w = (scores * decay[h, :, base:base + n]).astype(BF16)
            wts[h, trow, 0:n] = w
            ret[trow, cols] = dot_nn(w, pv[0:n, cols])
        return 0

    cuts = [heads * i // 4 for i in range(5)]
    lax.fori_loop(cuts[0], cuts[1], forward, 0)
    for o in range(1, count):
        w_copies[o - 1].wait_send()
        frm = lax.rem(me + count - o, count)
        remote(w_out, w_in.at[frm], w_ss.at[o], w_rs.at[frm], "dp", frm).wait_recv()
    mid = [across(st_in, p1_rs, p1_ss, 0, False, 0)]
    lax.fori_loop(cuts[1], cuts[2], forward, 0)
    mid.append(across(st_in, p1_rs, p1_ss, 0, False, 1))
    lax.fori_loop(cuts[2], cuts[3], forward, 0)
    p2 = prefix(st_in, st_ret, carry, p2_ss, p2_rs, 0, mid[0], False, 0)
    lax.fori_loop(cuts[3], cuts[4], forward, 0)
    p2 += prefix(st_in, st_ret, carry, p2_ss, p2_rs, 0, mid[1], False, 1)
    for copy in dy_copies:
        copy.wait()
    put(pdy, guest_of(blk_out[3], lambda level: blk_in[level, 3]))
    gather_wait(carry, st_ret, p2_ss, p2_rs)

    def cross(h, sums):
        cols = columns(h)
        part = dot_nn(pq[:, cols], carry[state_rows(h), :])
        r = ret[:, cols] + part * (twice(colb[heads + h]) * inv)
        ret[:, cols] = r
        s = gain[:, cols] * pdy[:, cols].astype(F32)
        sq = r * r
        sr = s * r
        return (sums[0] + sq[:, 0:128] + sq[:, 128:256], sums[1] + sr[:, 0:128] + sr[:, 128:256])

    zero = jnp.zeros((tokens, 128), F32)
    sums = lax.fori_loop(0, heads, cross, (zero, zero))
    sq_row = jnp.sum(jnp.transpose(sums[0]), axis=0, keepdims=True)
    in_row = jnp.sum(jnp.transpose(sums[1]), axis=0, keepdims=True)
    hs_out[...] = jnp.where(sub == 0, sq_row, in_row)
    h_copies = []
    for o in range(1, hcount):
        to = lax.rem(hme + o, hcount)
        copy = remote(hs_out, hs_in.at[hme], hs_ss.at[o], hs_rs.at[hme], "head", to)
        copy.start()
        h_copies.append(copy)
    both = hs_out[...]
    for o in range(1, hcount):
        frm = lax.rem(hme + hcount - o, hcount)
        remote(hs_out, hs_in.at[frm], hs_ss.at[o], hs_rs.at[frm], "head", frm).wait_recv()
        both = both + hs_in[frm]
    for copy in p1:
        copy.wait_send()
    recip = lax.rsqrt(both[0:1, :] * (1.0 / FEATURES) + EPSILON)
    coef = recip * recip * recip * both[1:2, :] * (1.0 / FEATURES)
    hs_cols = (to_column(recip, tokens), to_column(coef, tokens))
    segc[...] = hs_cols[0]
    dkin[:, 0:128] = hs_cols[1]

    def back_state(h, _):
        cols = columns(h)
        s = gain[:, cols] * pdy[:, cols].astype(F32)
        g = (twice(segc[...]) * s - twice(dkin[:, 0:128]) * ret[:, cols]).astype(BF16)
        grad[:, cols] = g
        gated = (g.astype(F32) * twice(colb[heads + h])).astype(BF16)
        st_out[state_rows(h), :] = (dot_tn(pq[:, cols], gated) * inv).astype(BF16)
        return 0

    lax.fori_loop(0, heads, back_state, 0)
    b1 = scatter(bk_in, b1_ss, b1_rs, 0) + scatter(bk_in, b1_ss, b1_rs, 1)

    def backward(h, _):
        cols = columns(h)
        for tb in range(tiles):
            n = (tb + 1) * TILE
            base = tb * (tb + 1) // 2 * TILE
            trow = pl.ds(tb * TILE, TILE)
            g = grad[trow, cols]
            scores = dot_nt(g, pv[0:n, cols])
            w = (scores * decay[h, :, base:base + n]).astype(BF16)
            gw[trow, 0:n] = w
            part = dot_nt(g, carry[state_rows(h), :])
            fc = twice(colb[heads + h, trow, :]) * inv
            pdy[trow, cols] = (dot_nn(w, pk[0:n, cols]) + fc * part).astype(BF16)
        for sb in range(tiles):
            lo = sb * TILE
            srow = pl.ds(lo, TILE)
            dkin[srow, cols] = dot_tn(gw[lo:, lo:lo + TILE], pq[lo:, cols])
            ret[srow, cols] = dot_tn(wts[h, lo:, lo:lo + TILE], grad[lo:, cols])
        return 0

    lax.fori_loop(cuts[0], cuts[1], backward, 0)
    back_mid = [across(bk_in, b1_rs, b1_ss, 1, True, 0)]
    lax.fori_loop(cuts[1], cuts[2], backward, 0)
    back_mid.append(across(bk_in, b1_rs, b1_ss, 1, True, 1))
    lax.fori_loop(cuts[2], cuts[3], backward, 0)
    b2 = prefix(bk_in, bk_ret, cback, b2_ss, b2_rs, 1, back_mid[0], True, 0)
    b2 += prefix(bk_in, bk_ret, cback, b2_ss, b2_rs, 1, back_mid[1], True, 1)
    lax.fori_loop(cuts[3], cuts[4], backward, 0)
    lv_out[0] = pick(pdy)
    lv_copies = to_partners(lv_out.at[0], lambda level: lv_in.at[level, 0], lv_ss, lv_rs, 0)

    def pick_wide(b, acc):
        at = pl.ds(pl.multiple_of(b * length, length), length)
        mask = widen(sel[at, :].astype(F32))
        return acc[0] + dkin[at, :] * mask, acc[1] + ret[at, :] * mask

    zero = jnp.zeros((length, width), F32)
    fin[0], fin[1] = lax.fori_loop(0, blocks, pick_wide, (zero, zero))
    gather_wait(cback, bk_ret, b2_ss, b2_rs)

    def finish_block(h, _):
        cols = columns(h)
        lc = twice(last_g[h])
        state = cback[state_rows(h), :]
        lv_out[1, :, cols] = (fin[0, :, cols] + lc * dot_nt(guest_kv[1, :, cols], state)).astype(BF16)
        lv_out[2, :, cols] = (fin[1, :, cols] + lc * dot_nn(guest_kv[0, :, cols], state)).astype(BF16)
        return 0

    lax.fori_loop(0, heads, finish_block, 0)
    lv_copies += to_partners(lv_out.at[1:3], lambda level: lv_in.at[level, 1:3], lv_ss, lv_rs, levels)

    def finish(h, _):
        cols = columns(h)
        lc = twice(colb[2 * heads + h])
        state = cback[state_rows(h), :]
        k = pk[:, cols]
        dk = dkin[:, cols] + lc * dot_nt(pv[:, cols], state)
        dv = ret[:, cols] + lc * dot_nn(k, state)
        pk[:, cols] = dk.astype(BF16)
        pv[:, cols] = dv.astype(BF16)
        return 0

    lax.fori_loop(0, heads, finish, 0)
    for copy in p2 + b1 + b2 + h_copies + mid + back_mid:
        copy.wait_send()
    for copy in lv_copies:
        copy.wait()
    for i in range(3):
        guest_out[i] = guest_of(lv_out[i], lambda level: lv_in[level, i])


def place_kernel(slots, guest, dq, dk, dv, oq, ok, ov, sem):
    slot = slots[lax.axis_index("dp")]
    per = 4
    chunk = per * BLOCK_LEN

    def one(c, _):
        inside = slot // per == c
        at = pl.multiple_of(c * chunk, chunk)
        for i, (src, dst) in enumerate(((dq, oq), (dk, ok), (dv, ov))):

            @pl.when(jnp.logical_not(inside))
            def _():
                rows = pl.ds(at, chunk)
                pltpu.make_async_copy(src.at[rows], dst.at[rows], sem.at[i]).start()

            @pl.when(inside)
            def _():
                for b in range(per):
                    rows = pl.ds(pl.multiple_of(at + b * BLOCK_LEN, BLOCK_LEN), BLOCK_LEN)

                    @pl.when(c * per + b == slot)
                    def _():
                        pltpu.make_async_copy(guest.at[i], dst.at[rows], sem.at[i]).start()

                    @pl.when(c * per + b != slot)
                    def _():
                        pltpu.make_async_copy(src.at[rows], dst.at[rows], sem.at[i]).start()

        return 0

    lax.fori_loop(0, dq.shape[0] // chunk, one, 0)
    for i, (src, dst) in enumerate(((dq, oq), (dk, ok), (dv, ov))):
        pltpu.make_async_copy(src, dst, sem.at[i]).wait()


def local(count, hcount, queries, keys, values, out_grad, norm_gain, table, index, lengths, partners, slots):
    tokens, width = queries.shape
    heads = table.shape[0]
    tiles = tokens // TILE
    levels = count.bit_length() - 1
    group = count // 2
    span = heads * HEAD_DIM // group
    smem = pl.BlockSpec(memory_space=pltpu.SMEM)
    vmem = pl.BlockSpec(memory_space=pltpu.VMEM)
    any_ = pl.BlockSpec(memory_space=pl.ANY)
    full = jax.ShapeDtypeStruct((tokens, width), BF16)
    V = pltpu.VMEM
    D = pltpu.SemaphoreType.DMA
    held = V((tokens, width), BF16)
    state = V((heads * HEAD_DIM, HEAD_DIM), BF16)
    part = V((group, span, HEAD_DIM), BF16)
    dq, dk, dv, guest = pl.pallas_call(
        functools.partial(main_kernel, count, hcount, heads, tokens),
        out_shape=(held, held, held, V((3, BLOCK_LEN, width), BF16)),
        in_specs=[smem, smem, smem, vmem, vmem, vmem, any_, any_, any_, any_],
        out_specs=(vmem, vmem, vmem, vmem),
        scratch_shapes=[
            held,
            V((heads, tokens, tokens), BF16),
            V((heads, TILE, tiles * (tiles + 1) // 2 * TILE), F32),
            V((tokens, tokens), BF16),
            V((tokens, width), F32), V((tokens, width), F32), V((tokens, width), BF16),
            V((3 * heads, tokens, 128), F32), V((tokens, 128), F32), V((8, tokens), F32),
            V((tokens, 128), BF16), V((tokens, 128), BF16),
            V((2, BLOCK_LEN, width), BF16), V((heads, BLOCK_LEN, 128), F32), V((2, BLOCK_LEN, width), F32),
            V((8, tokens), F32), V((levels, 8, tokens), F32),
            V((4, BLOCK_LEN, width), BF16), V((levels, 4, BLOCK_LEN, width), BF16),
            V((count, 8, 128), F32), V((8, 128), F32),
            state, part, part, state, part, part, state,
            V((4, span // 2, HEAD_DIM), BF16), V((4, span // 2, HEAD_DIM), BF16),
            V((8, tokens), F32), V((hcount, 8, tokens), F32),
            V((3, BLOCK_LEN, width), BF16), V((levels, 3, BLOCK_LEN, width), BF16),
            D((4,)), D((levels,)), D((levels,)), D((3 * levels,)), D((3 * levels,)),
            D((count,)), D((count,)), D((2 * group,)), D((2 * group,)), D((2 * group,)), D((2 * group,)),
            D((2 * group,)), D((2 * group,)), D((2 * group,)), D((2 * group,)), D((4,)), D((4,)),
            D((hcount,)), D((hcount,)), D((2 * levels,)), D((2 * levels,)),
        ],
        compiler_params=pltpu.CompilerParams(
            collective_id=0, has_side_effects=True, vmem_limit_bytes=50 * 1024 * 1024
        ),
    )(lengths, partners, slots, table, index, norm_gain.reshape(1, width), queries, keys, values, out_grad)

    kept = [pltpu.with_memory_space_constraint(a, pltpu.VMEM) for a in (guest, dq, dk, dv)]
    return pl.pallas_call(
        place_kernel,
        out_shape=(full, full, full),
        in_specs=[smem, vmem, vmem, vmem, vmem],
        out_specs=(any_, any_, any_),
        scratch_shapes=[D((3,))],
        compiler_params=pltpu.CompilerParams(vmem_limit_bytes=1024 * 1024),
    )(slots, *kept)


def solution(mesh):
    placed = (
        P("dp", "head"), P("dp", "head"), P("dp", "head"), P("dp", "head"),
        P("head"), P("head", None), P("head", "dp"), P(), P(), P(),
    )
    return jax.shard_map(
        functools.partial(local, mesh.shape["dp"], mesh.shape["head"]),
        mesh=mesh,
        in_specs=placed,
        out_specs=(P("dp", "head"), P("dp", "head"), P("dp", "head")),
        check_vma=False,
    )
```

```python
import functools

import jax
import jax.numpy as jnp
from jax import lax
from jax.experimental import pallas as pl
from jax.experimental.pallas import tpu as pltpu
from jax.sharding import PartitionSpec as P

HEAD_DIM = 256
BLOCK_LEN = 32
FEATURES = 4096
EPSILON = 1e-05
TILE = 256
MESH = pl.DeviceIdType.MESH
F32 = jnp.float32
BF16 = jnp.bfloat16


def dot_nt(a, b):
    return lax.dot_general(a, b, (((1,), (1,)), ((), ())), preferred_element_type=F32)


def dot_tn(a, b):
    return lax.dot_general(a, b, (((0,), (0,)), ((), ())), preferred_element_type=F32)


def dot_nn(a, b):
    return jnp.dot(a, b, preferred_element_type=F32)


def twice(col):
    return jnp.concatenate([col, col], axis=1)


def to_column(row, tokens):
    return jnp.transpose(jnp.broadcast_to(row, (128, tokens)))


def main_kernel(
    count, hcount, heads, tokens,
    lengths, partners, slots, table, index, gain, q_hbm, k_hbm, v_hbm, dy_hbm,
    pdy, pk, pv, guest_out,
    pq, wts, decay, gw, ret, dkin, grad, colb, segc, cum_s,
    sel, unsel, guest_kv, last_g, fin, bstate, rate_out, rate_in, blk_out, blk_in, w_in, w_out,
    st_out, st_in, st_ret, carry, bk_in, bk_ret, cback, mid_out, mid_in,
    hs_out, hs_in, lv_out, lv_in,
    in_sem, rate_ss, rate_rs, blk_ss, blk_rs, w_ss, w_rs,
    p1_ss, p1_rs, p2_ss, p2_rs, b1_ss, b1_rs, b2_ss, b2_rs, mid_ss, mid_rs, hs_ss, hs_rs, lv_ss, lv_rs,
):
    me = lax.axis_index("dp")
    hme = lax.axis_index("head")
    levels = count.bit_length() - 1
    length = BLOCK_LEN
    group = count // 2
    side = me // group
    base_row = side * group
    pos = me - base_row
    mate = me + group - 2 * group * side
    span = heads * HEAD_DIM // group
    sub_span = span // 2
    tiles = tokens // TILE
    width = heads * HEAD_DIM
    inv = 1.0 / HEAD_DIM

    loads = []
    for i, (src, dst) in enumerate(((k_hbm, pk), (v_hbm, pv), (q_hbm, pq), (dy_hbm, pdy))):
        copy = pltpu.make_async_copy(src, dst, in_sem.at[i])
        copy.start()
        loads.append(copy)

    barrier = pltpu.get_barrier_semaphore()
    for o in range(1, count):
        pl.semaphore_signal(barrier, inc=1, device_id={"dp": lax.rem(me + o, count)}, device_id_type=MESH)
    for o in range(1, hcount):
        pl.semaphore_signal(barrier, inc=1, device_id={"head": lax.rem(hme + o, hcount)}, device_id_type=MESH)

    idx = index[...]
    rate = jnp.zeros((heads, tokens), F32)
    for level in range(table.shape[1]):
        rate = jnp.where(idx == level, table[:, level:level + 1], rate)
    rate_out[...] = jnp.zeros((8, tokens), F32)
    rate_out[0:heads, :] = rate

    slot = slots[me]
    partner = partners[me]
    partner_slot = slot
    for d in range(count):
        partner_slot = jnp.where(partner == d, slots[d], partner_slot)
    pl.semaphore_wait(barrier, count - 1 + hcount - 1)

    def remote(src, dst, ss, rs, axis, to):
        return pltpu.make_async_remote_copy(
            src_ref=src, dst_ref=dst, send_sem=ss, recv_sem=rs,
            device_id={axis: to}, device_id_type=MESH,
        )

    def other(level):
        bit = 1 << level
        return me + bit - 2 * bit * (lax.rem(me // bit, 2))

    rate_copies = []
    for level in range(levels):
        copy = remote(rate_out, rate_in.at[level], rate_ss.at[level], rate_rs.at[level], "dp", other(level))
        copy.start()
        rate_copies.append(copy)

    blocks = tokens // length

    chosen = lax.broadcasted_iota(jnp.int32, (tokens, 128), 0) // length == jnp.full((tokens, 128), slot, jnp.int32)
    sel[...] = jnp.where(chosen, 1.0, 0.0).astype(BF16)
    unsel[...] = jnp.where(chosen, 0.0, 1.0).astype(BF16)

    def widen(mask):
        return jnp.concatenate([mask] * (width // 128), axis=1)

    def pick(ref):
        def one(b, acc):
            at = pl.ds(pl.multiple_of(b * length, length), length)
            return acc + ref[at, :] * widen(sel[at, :])

        return lax.fori_loop(0, blocks, one, jnp.zeros((length, width), BF16))

    def to_partners(out, inbox, ss, rs, first):
        copies = []
        for level in range(levels):
            copy = remote(out, inbox(level), ss.at[first + level], rs.at[first + level], "dp", other(level))
            copy.start()
            copies.append(copy)
        return copies

    def guest_of(own_block, inbox):
        block = own_block.astype(F32)
        for level in range(levels):
            match = jnp.full(block.shape, partner, jnp.int32) == other(level)
            block = jnp.where(match, inbox(level).astype(F32), block)
        return block.astype(BF16)

    def put(ref, block):
        def one(b, _):
            at = pl.ds(pl.multiple_of(b * length, length), length)
            ref[at, :] = ref[at, :] * widen(unsel[at, :]) + block * widen(sel[at, :])
            return 0

        lax.fori_loop(0, blocks, one, 0)

    packed = (pk, pv, pq, pdy)

    def load_and_pick(i):
        loads[i].wait()
        blk_out[i] = pick(packed[i])

    load_and_pick(0)
    load_and_pick(1)
    kv_copies = to_partners(blk_out.at[0:2], lambda level: blk_in.at[level, 0:2], blk_ss, blk_rs, 0)
    load_and_pick(2)
    q_copies = to_partners(blk_out.at[2], lambda level: blk_in.at[level, 2], blk_ss, blk_rs, levels)
    load_and_pick(3)

    lane = lax.broadcasted_iota(jnp.int32, (8, tokens), 1)
    sub = lax.broadcasted_iota(jnp.int32, (8, tokens), 0)
    flag = jnp.zeros((8, tokens), F32)
    start = jnp.int32(0)
    for n in range(lengths.shape[0]):
        flag = jnp.where(lane == start - me * tokens, 1.0, flag)
        start = start + lengths[n]

    own = rate_out[...]
    guest = own
    for level in range(levels):
        rate_copies[level].wait()
        guest = jnp.where(jnp.full((8, tokens), partner, jnp.int32) == other(level), rate_in[level], guest)
    shift = slot - partner_slot + blocks
    for bit in range(blocks.bit_length() - 1):
        here = (jnp.full((8, tokens), shift, jnp.int32) >> bit) & 1
        guest = jnp.where(here == 1, pltpu.roll(guest, length << bit, 1), guest)
    rows = jnp.where(lane // length == jnp.full((8, tokens), slot, jnp.int32), guest, own)
    cum = jnp.where(sub == heads, flag, rows)
    step = 1
    while step < tokens:
        cum = cum + jnp.where(lane >= step, pltpu.roll(cum, step, 1), 0.0)
        step *= 2
    cum_s[...] = cum
    seg = cum[heads:heads + 1, :]
    seg_last = cum[heads:heads + 1, tokens - 1:tokens]
    cum_last = cum[:, tokens - 1:tokens]
    first8 = jnp.where(seg == 0.0, jnp.exp(-cum), 0.0)
    last8 = jnp.where(seg == seg_last, jnp.exp(cum - cum_last), 0.0)
    whole8 = jnp.where(seg_last == 0.0, jnp.exp(-cum_last), 0.0)
    w_out[...] = jnp.broadcast_to(whole8, (8, 128))
    w_copies = []
    for o in range(1, count):
        to = lax.rem(me + o, count)
        copy = remote(w_out, w_in.at[me], w_ss.at[o], w_rs.at[me], "dp", to)
        copy.start()
        w_copies.append(copy)
    w_in[me] = w_out[...]
    for h in range(heads):
        colb[h] = to_column(cum[h:h + 1, :], tokens)
        colb[heads + h] = to_column(first8[h:h + 1, :], tokens)
        colb[2 * heads + h] = to_column(last8[h:h + 1, :], tokens)
    segc[...] = to_column(seg, tokens)

    def columns(h):
        return pl.ds(pl.multiple_of(h * HEAD_DIM, HEAD_DIM), HEAD_DIM)

    def state_rows(h):
        return pl.ds(pl.multiple_of(h * HEAD_DIM, HEAD_DIM), HEAD_DIM)

    def span_rows(j):
        return pl.ds(pl.multiple_of(j * span, span), span)

    def part_rows(j, c):
        return pl.ds(pl.multiple_of(j * span + c * sub_span, sub_span), sub_span)

    def half_rows(c):
        return pl.ds(c * sub_span, sub_span)

    def scatter(inbox, ss, rs, c):
        copies = []
        for o in range(1, group):
            to = lax.rem(pos + o, group)
            copy = remote(
                st_out.at[part_rows(to, c)], inbox.at[pos, half_rows(c)],
                ss.at[c * group + o], rs.at[c * group + pos], "dp", base_row + to,
            )
            copy.start()
            copies.append(copy)
        inbox[pos, half_rows(c), :] = st_out[part_rows(pos, c), :]
        return copies

    head_of_span = pos * span // HEAD_DIM

    def fold(inbox, run, reverse, outbox, c):
        def one(turn, run):
            d = group - 1 - turn if reverse else turn
            if outbox is not None:
                outbox[d, half_rows(c), :] = run.astype(BF16)
            w = w_in[base_row + d, pl.ds(head_of_span, 1), :]
            return twice(w) * run + inbox[d, half_rows(c), :].astype(F32)

        return lax.fori_loop(0, group, one, run)

    def across(inbox, rs, ss, which, reverse, c):
        for o in range(1, group):
            frm = lax.rem(pos + group - o, group)
            remote(
                st_out.at[part_rows(0, c)], inbox.at[frm, half_rows(c)],
                ss.at[c * group + o], rs.at[c * group + frm], "dp", base_row + frm,
            ).wait_recv()
        at = 2 * which + c
        mid_out[at] = fold(inbox, jnp.zeros((sub_span, HEAD_DIM), F32), reverse, None, c).astype(BF16)
        copy = remote(mid_out.at[at], mid_in.at[at], mid_ss.at[at], mid_rs.at[at], "dp", mate)
        copy.start()
        return copy

    def prefix(inbox, outbox, home, ss2, rs2, which, copy, reverse, c):
        copy.wait_recv()
        behind = jnp.full((sub_span, HEAD_DIM), side, jnp.int32) == (0 if reverse else 1)
        run = jnp.where(behind, mid_in[2 * which + c].astype(F32), 0.0)
        fold(inbox, run, reverse, outbox, c)
        copies = []
        for o in range(1, group):
            to = lax.rem(pos + o, group)
            out = remote(
                outbox.at[to, half_rows(c)], home.at[part_rows(pos, c)],
                ss2.at[c * group + o], rs2.at[c * group + pos], "dp", base_row + to,
            )
            out.start()
            copies.append(out)
        home[part_rows(pos, c), :] = outbox[pos, half_rows(c), :]
        return copies

    def gather_wait(home, outbox, ss2, rs2):
        for c in range(2):
            for o in range(1, group):
                frm = lax.rem(pos + group - o, group)
                remote(
                    outbox.at[0, half_rows(c)], home.at[part_rows(frm, c)],
                    ss2.at[c * group + o], rs2.at[c * group + frm], "dp", base_row + frm,
                ).wait_recv()

    def kept_state(h, _):
        last = colb[2 * heads + h]
        gated = (pv[:, columns(h)].astype(F32) * twice(last)).astype(BF16) * twice(unsel[...])
        dkin[state_rows(h), 0:HEAD_DIM] = dot_tn(pk[:, columns(h)], gated)

        def one(b, acc):
            at = pl.ds(pl.multiple_of(b * length, length), length)
            return acc + colb[2 * heads + h, at, :] * sel[at, :].astype(F32)

        last_g[h] = lax.fori_loop(0, blocks, one, jnp.zeros((length, 128), F32))
        return 0

    lax.fori_loop(0, heads, kept_state, 0)

    def make_decay(h, _):
        for tb in range(tiles):
            base = tb * (tb + 1) // 2 * TILE
            trow = pl.ds(tb * TILE, TILE)
            ct = twice(colb[h, trow, :])
            sc = twice(segc[trow, :])
            for sb in range(tb + 1):
                scol = pl.ds(sb * TILE, TILE)
                inside = cum_s[heads:heads + 1, scol] == sc
                if sb == tb:
                    r = lax.broadcasted_iota(jnp.int32, (TILE, TILE), 0)
                    c = lax.broadcasted_iota(jnp.int32, (TILE, TILE), 1)
                    inside = inside & (r >= c)
                value = jnp.exp(jnp.minimum(cum_s[pl.ds(h, 1), scol] - ct, 0.0)) * inv
                decay[h, :, base + sb * TILE:base + (sb + 1) * TILE] = jnp.where(inside, value, 0.0)
        return 0

    cuts = [heads * i // 4 for i in range(5)]
    for copy in kv_copies:
        copy.wait()
    for i in range(2):
        guest_kv[i] = guest_of(blk_out[i], lambda level: blk_in[level, i])

    def local_state(h, _):
        gated = (guest_kv[1, :, columns(h)].astype(F32) * twice(last_g[h])).astype(BF16)
        state = dkin[state_rows(h), 0:HEAD_DIM] + dot_tn(guest_kv[0, :, columns(h)], gated)
        st_out[state_rows(h), :] = state.astype(BF16)
        return 0

    lax.fori_loop(0, heads, local_state, 0)
    p1 = scatter(st_in, p1_ss, p1_rs, 0) + scatter(st_in, p1_ss, p1_rs, 1)
    dy_copies = to_partners(blk_out.at[3], lambda level: blk_in.at[level, 3], blk_ss, blk_rs, 2 * levels)
    lax.fori_loop(cuts[0], cuts[2], make_decay, 0)
    put(pk, guest_kv[0])
    put(pv, guest_kv[1])
    for copy in q_copies:
        copy.wait()
    put(pq, guest_of(blk_out[2], lambda level: blk_in[level, 2]))

    def forward(h, _):
        cols = columns(h)
        for tb in range(tiles):
            n = (tb + 1) * TILE
            base = tb * (tb + 1) // 2 * TILE
            trow = pl.ds(tb * TILE, TILE)
            scores = dot_nt(pq[trow, cols], pk[0:n, cols])
            w = (scores * decay[h, :, base:base + n]).astype(BF16)
            wts[h, trow, 0:n] = w
            ret[trow, cols] = dot_nn(w, pv[0:n, cols])
        return 0

    lax.fori_loop(cuts[0], cuts[1], forward, 0)
    for o in range(1, count):
        w_copies[o - 1].wait_send()
        frm = lax.rem(me + count - o, count)
        remote(w_out, w_in.at[frm], w_ss.at[o], w_rs.at[frm], "dp", frm).wait_recv()
    mid = [across(st_in, p1_rs, p1_ss, 0, False, 0)]
    lax.fori_loop(cuts[2], cuts[4], make_decay, 0)
    lax.fori_loop(cuts[1], cuts[2], forward, 0)
    mid.append(across(st_in, p1_rs, p1_ss, 0, False, 1))
    lax.fori_loop(cuts[2], cuts[3], forward, 0)
    p2 = prefix(st_in, st_ret, carry, p2_ss, p2_rs, 0, mid[0], False, 0)
    lax.fori_loop(cuts[3], cuts[4], forward, 0)
    p2 += prefix(st_in, st_ret, carry, p2_ss, p2_rs, 0, mid[1], False, 1)
    for copy in dy_copies:
        copy.wait()
    put(pdy, guest_of(blk_out[3], lambda level: blk_in[level, 3]))
    gather_wait(carry, st_ret, p2_ss, p2_rs)

    half = tokens // 2
    halves = (pl.ds(0, half), pl.ds(half, half))
    h_copies = []

    def send_sums(part):
        rows = halves[part]

        def cross(h, sums):
            cols = columns(h)
            r = dot_nn(pq[rows, cols], carry[state_rows(h), :])
            r = ret[rows, cols] + r * (twice(colb[heads + h, rows, :]) * inv)
            ret[rows, cols] = r
            s = gain[:, cols] * pdy[rows, cols].astype(F32)
            sq = r * r
            sr = s * r
            return (sums[0] + sq[:, 0:128] + sq[:, 128:256], sums[1] + sr[:, 0:128] + sr[:, 128:256])

        zero = jnp.zeros((half, 128), F32)
        sums = lax.fori_loop(0, heads, cross, (zero, zero))
        sq_row = jnp.sum(jnp.transpose(sums[0]), axis=0, keepdims=True)
        in_row = jnp.sum(jnp.transpose(sums[1]), axis=0, keepdims=True)
        top = lax.broadcasted_iota(jnp.int32, (8, half), 0) == 0
        hs_out[part] = jnp.where(top, sq_row, in_row)
        for o in range(1, hcount):
            to = lax.rem(hme + o, hcount)
            at = part * hcount
            copy = remote(
                hs_out.at[part], hs_in.at[part, hme], hs_ss.at[at + o], hs_rs.at[at + hme], "head", to
            )
            copy.start()
            h_copies.append(copy)

    def norm_columns(part):
        rows = halves[part]
        both = hs_out[part]
        for o in range(1, hcount):
            frm = lax.rem(hme + hcount - o, hcount)
            at = part * hcount
            remote(
                hs_out.at[part], hs_in.at[part, frm], hs_ss.at[at + o], hs_rs.at[at + frm], "head", frm
            ).wait_recv()
            both = both + hs_in[part, frm]
        recip = lax.rsqrt(both[0:1, :] * (1.0 / FEATURES) + EPSILON)
        coef = recip * recip * recip * both[1:2, :] * (1.0 / FEATURES)
        segc[rows, :] = to_column(recip, half)
        dkin[rows, 0:128] = to_column(coef, half)

    def back_state(part):
        rows = halves[part]

        def one(h, _):
            cols = columns(h)
            s = gain[:, cols] * pdy[rows, cols].astype(F32)
            g = (twice(segc[rows, :]) * s - twice(dkin[rows, 0:128]) * ret[rows, cols]).astype(BF16)
            grad[rows, cols] = g
            gated = (g.astype(F32) * twice(colb[heads + h, rows, :])).astype(BF16)
            state = dot_tn(pq[rows, cols], gated)
            if part == 0:
                bstate[state_rows(h), :] = state
            else:
                st_out[state_rows(h), :] = ((bstate[state_rows(h), :] + state) * inv).astype(BF16)
            return 0

        lax.fori_loop(0, heads, one, 0)

    send_sums(0)
    send_sums(1)
    for copy in p1:
        copy.wait_send()
    norm_columns(0)
    back_state(0)
    norm_columns(1)
    back_state(1)
    b1 = scatter(bk_in, b1_ss, b1_rs, 0) + scatter(bk_in, b1_ss, b1_rs, 1)

    def backward(h, _):
        cols = columns(h)
        for tb in range(tiles):
            n = (tb + 1) * TILE
            base = tb * (tb + 1) // 2 * TILE
            trow = pl.ds(tb * TILE, TILE)
            g = grad[trow, cols]
            scores = dot_nt(g, pv[0:n, cols])
            w = (scores * decay[h, :, base:base + n]).astype(BF16)
            gw[trow, 0:n] = w
            part = dot_nt(g, carry[state_rows(h), :])
            fc = twice(colb[heads + h, trow, :]) * inv
            pdy[trow, cols] = (dot_nn(w, pk[0:n, cols]) + fc * part).astype(BF16)
        for sb in range(tiles):
            lo = sb * TILE
            srow = pl.ds(lo, TILE)
            dkin[srow, cols] = dot_tn(gw[lo:, lo:lo + TILE], pq[lo:, cols])
            ret[srow, cols] = dot_tn(wts[h, lo:, lo:lo + TILE], grad[lo:, cols])
        return 0

    lax.fori_loop(cuts[0], cuts[1], backward, 0)
    back_mid = [across(bk_in, b1_rs, b1_ss, 1, True, 0)]
    lax.fori_loop(cuts[1], cuts[2], backward, 0)
    back_mid.append(across(bk_in, b1_rs, b1_ss, 1, True, 1))
    lax.fori_loop(cuts[2], cuts[3], backward, 0)
    b2 = prefix(bk_in, bk_ret, cback, b2_ss, b2_rs, 1, back_mid[0], True, 0)
    b2 += prefix(bk_in, bk_ret, cback, b2_ss, b2_rs, 1, back_mid[1], True, 1)
    lax.fori_loop(cuts[3], cuts[4], backward, 0)
    lv_out[0] = pick(pdy)
    lv_copies = to_partners(lv_out.at[0], lambda level: lv_in.at[level, 0], lv_ss, lv_rs, 0)

    def pick_wide(b, acc):
        at = pl.ds(pl.multiple_of(b * length, length), length)
        mask = widen(sel[at, :].astype(F32))
        return acc[0] + dkin[at, :] * mask, acc[1] + ret[at, :] * mask

    zero = jnp.zeros((length, width), F32)
    fin[0], fin[1] = lax.fori_loop(0, blocks, pick_wide, (zero, zero))
    gather_wait(cback, bk_ret, b2_ss, b2_rs)

    def finish_block(h, _):
        cols = columns(h)
        lc = twice(last_g[h])
        state = cback[state_rows(h), :]
        lv_out[1, :, cols] = (fin[0, :, cols] + lc * dot_nt(guest_kv[1, :, cols], state)).astype(BF16)
        lv_out[2, :, cols] = (fin[1, :, cols] + lc * dot_nn(guest_kv[0, :, cols], state)).astype(BF16)
        return 0

    lax.fori_loop(0, heads, finish_block, 0)
    lv_copies += to_partners(lv_out.at[1:3], lambda level: lv_in.at[level, 1:3], lv_ss, lv_rs, levels)

    def finish(h, _):
        cols = columns(h)
        lc = twice(colb[2 * heads + h])
        state = cback[state_rows(h), :]
        k = pk[:, cols]
        dk = dkin[:, cols] + lc * dot_nt(pv[:, cols], state)
        dv = ret[:, cols] + lc * dot_nn(k, state)
        pk[:, cols] = dk.astype(BF16)
        pv[:, cols] = dv.astype(BF16)
        return 0

    lax.fori_loop(0, heads, finish, 0)
    for copy in p2 + b1 + b2 + h_copies + mid + back_mid:
        copy.wait_send()
    for copy in lv_copies:
        copy.wait()
    for i in range(3):
        guest_out[i] = guest_of(lv_out[i], lambda level: lv_in[level, i])


def place_kernel(slots, guest, dq, dk, dv, oq, ok, ov, sem):
    slot = slots[lax.axis_index("dp")]
    per = 4
    chunk = per * BLOCK_LEN

    def one(c, _):
        inside = slot // per == c
        at = pl.multiple_of(c * chunk, chunk)
        for i, (src, dst) in enumerate(((dq, oq), (dk, ok), (dv, ov))):

            @pl.when(jnp.logical_not(inside))
            def _():
                rows = pl.ds(at, chunk)
                pltpu.make_async_copy(src.at[rows], dst.at[rows], sem.at[i]).start()

            @pl.when(inside)
            def _():
                for b in range(per):
                    rows = pl.ds(pl.multiple_of(at + b * BLOCK_LEN, BLOCK_LEN), BLOCK_LEN)

                    @pl.when(c * per + b == slot)
                    def _():
                        pltpu.make_async_copy(guest.at[i], dst.at[rows], sem.at[i]).start()

                    @pl.when(c * per + b != slot)
                    def _():
                        pltpu.make_async_copy(src.at[rows], dst.at[rows], sem.at[i]).start()

        return 0

    lax.fori_loop(0, dq.shape[0] // chunk, one, 0)
    for i, (src, dst) in enumerate(((dq, oq), (dk, ok), (dv, ov))):
        pltpu.make_async_copy(src, dst, sem.at[i]).wait()


def local(count, hcount, queries, keys, values, out_grad, norm_gain, table, index, lengths, partners, slots):
    tokens, width = queries.shape
    heads = table.shape[0]
    tiles = tokens // TILE
    levels = count.bit_length() - 1
    group = count // 2
    span = heads * HEAD_DIM // group
    smem = pl.BlockSpec(memory_space=pltpu.SMEM)
    vmem = pl.BlockSpec(memory_space=pltpu.VMEM)
    any_ = pl.BlockSpec(memory_space=pl.ANY)
    full = jax.ShapeDtypeStruct((tokens, width), BF16)
    V = pltpu.VMEM
    D = pltpu.SemaphoreType.DMA
    held = V((tokens, width), BF16)
    state = V((heads * HEAD_DIM, HEAD_DIM), BF16)
    part = V((group, span, HEAD_DIM), BF16)
    dq, dk, dv, guest = pl.pallas_call(
        functools.partial(main_kernel, count, hcount, heads, tokens),
        out_shape=(held, held, held, V((3, BLOCK_LEN, width), BF16)),
        in_specs=[smem, smem, smem, vmem, vmem, vmem, any_, any_, any_, any_],
        out_specs=(vmem, vmem, vmem, vmem),
        scratch_shapes=[
            held,
            V((heads, tokens, tokens), BF16),
            V((heads, TILE, tiles * (tiles + 1) // 2 * TILE), F32),
            V((tokens, tokens), BF16),
            V((tokens, width), F32), V((tokens, width), F32), V((tokens, width), BF16),
            V((3 * heads, tokens, 128), F32), V((tokens, 128), F32), V((8, tokens), F32),
            V((tokens, 128), BF16), V((tokens, 128), BF16),
            V((2, BLOCK_LEN, width), BF16), V((heads, BLOCK_LEN, 128), F32), V((2, BLOCK_LEN, width), F32),
            V((heads * HEAD_DIM, HEAD_DIM), F32),
            V((8, tokens), F32), V((levels, 8, tokens), F32),
            V((4, BLOCK_LEN, width), BF16), V((levels, 4, BLOCK_LEN, width), BF16),
            V((count, 8, 128), F32), V((8, 128), F32),
            state, part, part, state, part, part, state,
            V((4, span // 2, HEAD_DIM), BF16), V((4, span // 2, HEAD_DIM), BF16),
            V((2, 8, tokens // 2), F32), V((2, hcount, 8, tokens // 2), F32),
            V((3, BLOCK_LEN, width), BF16), V((levels, 3, BLOCK_LEN, width), BF16),
            D((4,)), D((levels,)), D((levels,)), D((3 * levels,)), D((3 * levels,)),
            D((count,)), D((count,)), D((2 * group,)), D((2 * group,)), D((2 * group,)), D((2 * group,)),
            D((2 * group,)), D((2 * group,)), D((2 * group,)), D((2 * group,)), D((4,)), D((4,)),
            D((2 * hcount,)), D((2 * hcount,)), D((2 * levels,)), D((2 * levels,)),
        ],
        compiler_params=pltpu.CompilerParams(
            collective_id=0, has_side_effects=True, vmem_limit_bytes=50 * 1024 * 1024
        ),
    )(lengths, partners, slots, table, index, norm_gain.reshape(1, width), queries, keys, values, out_grad)

    kept = [pltpu.with_memory_space_constraint(a, pltpu.VMEM) for a in (guest, dq, dk, dv)]
    return pl.pallas_call(
        place_kernel,
        out_shape=(full, full, full),
        in_specs=[smem, vmem, vmem, vmem, vmem],
        out_specs=(any_, any_, any_),
        scratch_shapes=[D((3,))],
        compiler_params=pltpu.CompilerParams(vmem_limit_bytes=1024 * 1024),
    )(slots, *kept)


def solution(mesh):
    placed = (
        P("dp", "head"), P("dp", "head"), P("dp", "head"), P("dp", "head"),
        P("head"), P("head", None), P("head", "dp"), P(), P(), P(),
    )
    return jax.shard_map(
        functools.partial(local, mesh.shape["dp"], mesh.shape["head"]),
        mesh=mesh,
        in_specs=placed,
        out_specs=(P("dp", "head"), P("dp", "head"), P("dp", "head")),
        check_vma=False,
    )
```

```python
import functools

import jax
import jax.numpy as jnp
from jax import lax
from jax.experimental import pallas as pl
from jax.experimental.pallas import tpu as pltpu
from jax.sharding import PartitionSpec as P

HEAD_DIM = 256
BLOCK_LEN = 32
FEATURES = 4096
EPSILON = 1e-05
TILE = 256
MESH = pl.DeviceIdType.MESH
F32 = jnp.float32
BF16 = jnp.bfloat16


def dot_nt(a, b):
    return lax.dot_general(a, b, (((1,), (1,)), ((), ())), preferred_element_type=F32)


def dot_tn(a, b):
    return lax.dot_general(a, b, (((0,), (0,)), ((), ())), preferred_element_type=F32)


def dot_nn(a, b):
    return jnp.dot(a, b, preferred_element_type=F32)


def twice(col):
    return jnp.concatenate([col, col], axis=1)


def to_column(row, tokens):
    return jnp.transpose(jnp.broadcast_to(row, (128, tokens)))


def main_kernel(
    count, hcount, heads, tokens,
    lengths, partners, slots, table, index, gain, q_hbm, k_hbm, v_hbm, dy_hbm,
    pdy, pk, pv, guest_out,
    pq, wts, decay, gw, ret, dkin, grad, colb, segc, cum_s,
    sel, unsel, guest_kv, last_g, fin, bstate, rate_out, rate_in, blk_out, blk_in, w_in, w_out,
    st_out, st_in, st_ret, carry, bk_in, bk_ret, cback, mid_out, mid_in,
    hs_out, hs_in, lv_out, lv_in,
    in_sem, rate_ss, rate_rs, blk_ss, blk_rs, w_ss, w_rs,
    p1_ss, p1_rs, p2_ss, p2_rs, b1_ss, b1_rs, b2_ss, b2_rs, mid_ss, mid_rs, hs_ss, hs_rs, lv_ss, lv_rs,
):
    me = lax.axis_index("dp")
    hme = lax.axis_index("head")
    levels = count.bit_length() - 1
    length = BLOCK_LEN
    group = count // 2
    side = me // group
    base_row = side * group
    pos = me - base_row
    mate = me + group - 2 * group * side
    span = heads * HEAD_DIM // group
    sub_span = span // 2
    tiles = tokens // TILE
    width = heads * HEAD_DIM
    inv = 1.0 / HEAD_DIM

    loads = []
    for i, (src, dst) in enumerate(((k_hbm, pk), (v_hbm, pv), (q_hbm, pq), (dy_hbm, pdy))):
        copy = pltpu.make_async_copy(src, dst, in_sem.at[i])
        copy.start()
        loads.append(copy)

    barrier = pltpu.get_barrier_semaphore()
    for o in range(1, count):
        pl.semaphore_signal(barrier, inc=1, device_id={"dp": lax.rem(me + o, count)}, device_id_type=MESH)
    for o in range(1, hcount):
        pl.semaphore_signal(barrier, inc=1, device_id={"head": lax.rem(hme + o, hcount)}, device_id_type=MESH)

    idx = index[...]
    rate = jnp.zeros((heads, tokens), F32)
    for level in range(table.shape[1]):
        rate = jnp.where(idx == level, table[:, level:level + 1], rate)
    rate_out[...] = jnp.zeros((8, tokens), F32)
    rate_out[0:heads, :] = rate

    slot = slots[me]
    partner = partners[me]
    partner_slot = slot
    for d in range(count):
        partner_slot = jnp.where(partner == d, slots[d], partner_slot)
    pl.semaphore_wait(barrier, count - 1 + hcount - 1)

    def remote(src, dst, ss, rs, axis, to):
        return pltpu.make_async_remote_copy(
            src_ref=src, dst_ref=dst, send_sem=ss, recv_sem=rs,
            device_id={axis: to}, device_id_type=MESH,
        )

    def other(level):
        bit = 1 << level
        return me + bit - 2 * bit * (lax.rem(me // bit, 2))

    rate_copies = []
    for level in range(levels):
        copy = remote(rate_out, rate_in.at[level], rate_ss.at[level], rate_rs.at[level], "dp", other(level))
        copy.start()
        rate_copies.append(copy)

    blocks = tokens // length

    chosen = lax.broadcasted_iota(jnp.int32, (tokens, 128), 0) // length == jnp.full((tokens, 128), slot, jnp.int32)
    sel[...] = jnp.where(chosen, 1.0, 0.0).astype(BF16)
    unsel[...] = jnp.where(chosen, 0.0, 1.0).astype(BF16)

    def widen(mask):
        return jnp.concatenate([mask] * (width // 128), axis=1)

    def pick(ref):
        def one(b, acc):
            at = pl.ds(pl.multiple_of(b * length, length), length)
            return acc + ref[at, :] * widen(sel[at, :])

        return lax.fori_loop(0, blocks, one, jnp.zeros((length, width), BF16))

    def to_partners(out, inbox, ss, rs, first):
        copies = []
        for level in range(levels):
            copy = remote(out, inbox(level), ss.at[first + level], rs.at[first + level], "dp", other(level))
            copy.start()
            copies.append(copy)
        return copies

    def guest_of(own_block, inbox):
        block = own_block.astype(F32)
        for level in range(levels):
            match = jnp.full(block.shape, partner, jnp.int32) == other(level)
            block = jnp.where(match, inbox(level).astype(F32), block)
        return block.astype(BF16)

    def put(ref, block):
        def one(b, _):
            at = pl.ds(pl.multiple_of(b * length, length), length)
            ref[at, :] = ref[at, :] * widen(unsel[at, :]) + block * widen(sel[at, :])
            return 0

        lax.fori_loop(0, blocks, one, 0)

    packed = (pk, pv, pq, pdy)

    def load_and_pick(i):
        loads[i].wait()
        blk_out[i] = pick(packed[i])

    load_and_pick(0)
    load_and_pick(1)
    kv_copies = to_partners(blk_out.at[0:2], lambda level: blk_in.at[level, 0:2], blk_ss, blk_rs, 0)
    load_and_pick(2)
    q_copies = to_partners(blk_out.at[2], lambda level: blk_in.at[level, 2], blk_ss, blk_rs, levels)
    load_and_pick(3)

    lane = lax.broadcasted_iota(jnp.int32, (8, tokens), 1)
    sub = lax.broadcasted_iota(jnp.int32, (8, tokens), 0)
    flag = jnp.zeros((8, tokens), F32)
    start = jnp.int32(0)
    for n in range(lengths.shape[0]):
        flag = jnp.where(lane == start - me * tokens, 1.0, flag)
        start = start + lengths[n]

    own = rate_out[...]
    guest = own
    for level in range(levels):
        rate_copies[level].wait()
        guest = jnp.where(jnp.full((8, tokens), partner, jnp.int32) == other(level), rate_in[level], guest)
    shift = slot - partner_slot + blocks
    for bit in range(blocks.bit_length() - 1):
        here = (jnp.full((8, tokens), shift, jnp.int32) >> bit) & 1
        guest = jnp.where(here == 1, pltpu.roll(guest, length << bit, 1), guest)
    rows = jnp.where(lane // length == jnp.full((8, tokens), slot, jnp.int32), guest, own)
    cum = jnp.where(sub == heads, flag, rows)
    step = 1
    while step < tokens:
        cum = cum + jnp.where(lane >= step, pltpu.roll(cum, step, 1), 0.0)
        step *= 2
    cum_s[...] = cum
    seg = cum[heads:heads + 1, :]
    seg_last = cum[heads:heads + 1, tokens - 1:tokens]
    cum_last = cum[:, tokens - 1:tokens]
    first8 = jnp.where(seg == 0.0, jnp.exp(-cum), 0.0)
    last8 = jnp.where(seg == seg_last, jnp.exp(cum - cum_last), 0.0)
    whole8 = jnp.where(seg_last == 0.0, jnp.exp(-cum_last), 0.0)
    w_out[...] = jnp.broadcast_to(whole8, (8, 128))
    w_copies = []
    for o in range(1, count):
        to = lax.rem(me + o, count)
        copy = remote(w_out, w_in.at[me], w_ss.at[o], w_rs.at[me], "dp", to)
        copy.start()
        w_copies.append(copy)
    w_in[me] = w_out[...]
    for h in range(heads):
        colb[2 * heads + h] = to_column(last8[h:h + 1, :], tokens)

    def columns(h):
        return pl.ds(pl.multiple_of(h * HEAD_DIM, HEAD_DIM), HEAD_DIM)

    def state_rows(h):
        return pl.ds(pl.multiple_of(h * HEAD_DIM, HEAD_DIM), HEAD_DIM)

    def span_rows(j):
        return pl.ds(pl.multiple_of(j * span, span), span)

    def part_rows(j, c):
        return pl.ds(pl.multiple_of(j * span + c * sub_span, sub_span), sub_span)

    def half_rows(c):
        return pl.ds(c * sub_span, sub_span)

    def scatter(inbox, ss, rs, c):
        copies = []
        for o in range(1, group):
            to = lax.rem(pos + o, group)
            copy = remote(
                st_out.at[part_rows(to, c)], inbox.at[pos, half_rows(c)],
                ss.at[c * group + o], rs.at[c * group + pos], "dp", base_row + to,
            )
            copy.start()
            copies.append(copy)
        inbox[pos, half_rows(c), :] = st_out[part_rows(pos, c), :]
        return copies

    head_of_span = pos * span // HEAD_DIM

    def fold(inbox, run, reverse, outbox, c):
        def one(turn, run):
            d = group - 1 - turn if reverse else turn
            if outbox is not None:
                outbox[d, half_rows(c), :] = run.astype(BF16)
            w = w_in[base_row + d, pl.ds(head_of_span, 1), :]
            return twice(w) * run + inbox[d, half_rows(c), :].astype(F32)

        return lax.fori_loop(0, group, one, run)

    def across(inbox, rs, ss, which, reverse, c):
        for o in range(1, group):
            frm = lax.rem(pos + group - o, group)
            remote(
                st_out.at[part_rows(0, c)], inbox.at[frm, half_rows(c)],
                ss.at[c * group + o], rs.at[c * group + frm], "dp", base_row + frm,
            ).wait_recv()
        at = 2 * which + c
        mid_out[at] = fold(inbox, jnp.zeros((sub_span, HEAD_DIM), F32), reverse, None, c).astype(BF16)
        copy = remote(mid_out.at[at], mid_in.at[at], mid_ss.at[at], mid_rs.at[at], "dp", mate)
        copy.start()
        return copy

    def prefix(inbox, outbox, home, ss2, rs2, which, copy, reverse, c):
        copy.wait_recv()
        behind = jnp.full((sub_span, HEAD_DIM), side, jnp.int32) == (0 if reverse else 1)
        run = jnp.where(behind, mid_in[2 * which + c].astype(F32), 0.0)
        fold(inbox, run, reverse, outbox, c)
        copies = []
        for o in range(1, group):
            to = lax.rem(pos + o, group)
            out = remote(
                outbox.at[to, half_rows(c)], home.at[part_rows(pos, c)],
                ss2.at[c * group + o], rs2.at[c * group + pos], "dp", base_row + to,
            )
            out.start()
            copies.append(out)
        home[part_rows(pos, c), :] = outbox[pos, half_rows(c), :]
        return copies

    def gather_wait(home, outbox, ss2, rs2):
        for c in range(2):
            for o in range(1, group):
                frm = lax.rem(pos + group - o, group)
                remote(
                    outbox.at[0, half_rows(c)], home.at[part_rows(frm, c)],
                    ss2.at[c * group + o], rs2.at[c * group + frm], "dp", base_row + frm,
                ).wait_recv()

    def kept_state(h, _):
        last = colb[2 * heads + h]
        gated = (pv[:, columns(h)].astype(F32) * twice(last)).astype(BF16) * twice(unsel[...])
        dkin[state_rows(h), 0:HEAD_DIM] = dot_tn(pk[:, columns(h)], gated)

        def one(b, acc):
            at = pl.ds(pl.multiple_of(b * length, length), length)
            return acc + colb[2 * heads + h, at, :] * sel[at, :].astype(F32)

        last_g[h] = lax.fori_loop(0, blocks, one, jnp.zeros((length, 128), F32))
        return 0

    lax.fori_loop(0, heads, kept_state, 0)

    def make_decay(h, _):
        for tb in range(tiles):
            base = tb * (tb + 1) // 2 * TILE
            trow = pl.ds(tb * TILE, TILE)
            ct = twice(colb[h, trow, :])
            sc = twice(segc[trow, :])
            for sb in range(tb + 1):
                scol = pl.ds(sb * TILE, TILE)
                inside = cum_s[heads:heads + 1, scol] == sc
                if sb == tb:
                    r = lax.broadcasted_iota(jnp.int32, (TILE, TILE), 0)
                    c = lax.broadcasted_iota(jnp.int32, (TILE, TILE), 1)
                    inside = inside & (r >= c)
                value = jnp.exp(jnp.minimum(cum_s[pl.ds(h, 1), scol] - ct, 0.0)) * inv
                decay[h, :, base + sb * TILE:base + (sb + 1) * TILE] = jnp.where(inside, value, 0.0)
        return 0

    cuts = [heads * i // 4 for i in range(5)]
    for copy in kv_copies:
        copy.wait()
    for i in range(2):
        guest_kv[i] = guest_of(blk_out[i], lambda level: blk_in[level, i])

    def local_state(h, _):
        gated = (guest_kv[1, :, columns(h)].astype(F32) * twice(last_g[h])).astype(BF16)
        state = dkin[state_rows(h), 0:HEAD_DIM] + dot_tn(guest_kv[0, :, columns(h)], gated)
        st_out[state_rows(h), :] = state.astype(BF16)
        return 0

    lax.fori_loop(0, heads, local_state, 0)
    p1 = scatter(st_in, p1_ss, p1_rs, 0) + scatter(st_in, p1_ss, p1_rs, 1)
    dy_copies = to_partners(blk_out.at[3], lambda level: blk_in.at[level, 3], blk_ss, blk_rs, 2 * levels)
    for h in range(heads):
        colb[h] = to_column(cum[h:h + 1, :], tokens)
        colb[heads + h] = to_column(first8[h:h + 1, :], tokens)
    segc[...] = to_column(seg, tokens)
    lax.fori_loop(cuts[0], cuts[2], make_decay, 0)
    put(pk, guest_kv[0])
    put(pv, guest_kv[1])
    for copy in q_copies:
        copy.wait()
    put(pq, guest_of(blk_out[2], lambda level: blk_in[level, 2]))

    def forward(h, _):
        cols = columns(h)
        for tb in range(tiles):
            n = (tb + 1) * TILE
            base = tb * (tb + 1) // 2 * TILE
            trow = pl.ds(tb * TILE, TILE)
            scores = dot_nt(pq[trow, cols], pk[0:n, cols])
            w = (scores * decay[h, :, base:base + n]).astype(BF16)
            wts[h, trow, 0:n] = w
            ret[trow, cols] = dot_nn(w, pv[0:n, cols])
        return 0

    lax.fori_loop(cuts[0], cuts[1], forward, 0)
    for o in range(1, count):
        w_copies[o - 1].wait_send()
        frm = lax.rem(me + count - o, count)
        remote(w_out, w_in.at[frm], w_ss.at[o], w_rs.at[frm], "dp", frm).wait_recv()
    mid = [across(st_in, p1_rs, p1_ss, 0, False, 0)]
    lax.fori_loop(cuts[2], cuts[4], make_decay, 0)
    lax.fori_loop(cuts[1], cuts[2], forward, 0)
    mid.append(across(st_in, p1_rs, p1_ss, 0, False, 1))
    lax.fori_loop(cuts[2], cuts[3], forward, 0)
    p2 = prefix(st_in, st_ret, carry, p2_ss, p2_rs, 0, mid[0], False, 0)
    lax.fori_loop(cuts[3], cuts[4], forward, 0)
    p2 += prefix(st_in, st_ret, carry, p2_ss, p2_rs, 0, mid[1], False, 1)
    for copy in dy_copies:
        copy.wait()
    put(pdy, guest_of(blk_out[3], lambda level: blk_in[level, 3]))
    gather_wait(carry, st_ret, p2_ss, p2_rs)

    half = tokens // 2
    halves = (pl.ds(0, half), pl.ds(half, half))
    h_copies = []

    def send_sums(part):
        rows = halves[part]

        def cross(h, sums):
            cols = columns(h)
            r = dot_nn(pq[rows, cols], carry[state_rows(h), :])
            r = ret[rows, cols] + r * (twice(colb[heads + h, rows, :]) * inv)
            ret[rows, cols] = r
            s = gain[:, cols] * pdy[rows, cols].astype(F32)
            sq = r * r
            sr = s * r
            return (sums[0] + sq[:, 0:128] + sq[:, 128:256], sums[1] + sr[:, 0:128] + sr[:, 128:256])

        zero = jnp.zeros((half, 128), F32)
        sums = lax.fori_loop(0, heads, cross, (zero, zero))
        sq_row = jnp.sum(jnp.transpose(sums[0]), axis=0, keepdims=True)
        in_row = jnp.sum(jnp.transpose(sums[1]), axis=0, keepdims=True)
        top = lax.broadcasted_iota(jnp.int32, (8, half), 0) == 0
        hs_out[part] = jnp.where(top, sq_row, in_row)
        for o in range(1, hcount):
            to = lax.rem(hme + o, hcount)
            at = part * hcount
            copy = remote(
                hs_out.at[part], hs_in.at[part, hme], hs_ss.at[at + o], hs_rs.at[at + hme], "head", to
            )
            copy.start()
            h_copies.append(copy)

    def norm_columns(part):
        rows = halves[part]
        both = hs_out[part]
        for o in range(1, hcount):
            frm = lax.rem(hme + hcount - o, hcount)
            at = part * hcount
            remote(
                hs_out.at[part], hs_in.at[part, frm], hs_ss.at[at + o], hs_rs.at[at + frm], "head", frm
            ).wait_recv()
            both = both + hs_in[part, frm]
        recip = lax.rsqrt(both[0:1, :] * (1.0 / FEATURES) + EPSILON)
        coef = recip * recip * recip * both[1:2, :] * (1.0 / FEATURES)
        segc[rows, :] = to_column(recip, half)
        dkin[rows, 0:128] = to_column(coef, half)

    def back_state(part):
        rows = halves[part]

        def one(h, _):
            cols = columns(h)
            s = gain[:, cols] * pdy[rows, cols].astype(F32)
            g = (twice(segc[rows, :]) * s - twice(dkin[rows, 0:128]) * ret[rows, cols]).astype(BF16)
            grad[rows, cols] = g
            gated = (g.astype(F32) * twice(colb[heads + h, rows, :])).astype(BF16)
            state = dot_tn(pq[rows, cols], gated)
            if part == 0:
                bstate[state_rows(h), :] = state
            else:
                st_out[state_rows(h), :] = ((bstate[state_rows(h), :] + state) * inv).astype(BF16)
            return 0

        lax.fori_loop(0, heads, one, 0)

    send_sums(0)
    send_sums(1)
    for copy in p1:
        copy.wait_send()
    norm_columns(0)
    back_state(0)
    norm_columns(1)
    back_state(1)
    b1 = scatter(bk_in, b1_ss, b1_rs, 0) + scatter(bk_in, b1_ss, b1_rs, 1)

    def backward(h, _):
        cols = columns(h)
        for tb in range(tiles):
            n = (tb + 1) * TILE
            base = tb * (tb + 1) // 2 * TILE
            trow = pl.ds(tb * TILE, TILE)
            g = grad[trow, cols]
            scores = dot_nt(g, pv[0:n, cols])
            w = (scores * decay[h, :, base:base + n]).astype(BF16)
            gw[trow, 0:n] = w
            part = dot_nt(g, carry[state_rows(h), :])
            fc = twice(colb[heads + h, trow, :]) * inv
            pdy[trow, cols] = (dot_nn(w, pk[0:n, cols]) + fc * part).astype(BF16)
        for sb in range(tiles):
            lo = sb * TILE
            srow = pl.ds(lo, TILE)
            dkin[srow, cols] = dot_tn(gw[lo:, lo:lo + TILE], pq[lo:, cols])
            ret[srow, cols] = dot_tn(wts[h, lo:, lo:lo + TILE], grad[lo:, cols])
        return 0

    lax.fori_loop(cuts[0], cuts[1], backward, 0)
    back_mid = [across(bk_in, b1_rs, b1_ss, 1, True, 0)]
    lax.fori_loop(cuts[1], cuts[2], backward, 0)
    back_mid.append(across(bk_in, b1_rs, b1_ss, 1, True, 1))
    lax.fori_loop(cuts[2], cuts[3], backward, 0)
    b2 = prefix(bk_in, bk_ret, cback, b2_ss, b2_rs, 1, back_mid[0], True, 0)
    b2 += prefix(bk_in, bk_ret, cback, b2_ss, b2_rs, 1, back_mid[1], True, 1)
    lax.fori_loop(cuts[3], cuts[4], backward, 0)
    lv_out[0] = pick(pdy)
    lv_copies = to_partners(lv_out.at[0], lambda level: lv_in.at[level, 0], lv_ss, lv_rs, 0)

    def pick_wide(b, acc):
        at = pl.ds(pl.multiple_of(b * length, length), length)
        mask = widen(sel[at, :].astype(F32))
        return acc[0] + dkin[at, :] * mask, acc[1] + ret[at, :] * mask

    zero = jnp.zeros((length, width), F32)
    fin[0], fin[1] = lax.fori_loop(0, blocks, pick_wide, (zero, zero))
    gather_wait(cback, bk_ret, b2_ss, b2_rs)

    def finish_block(h, _):
        cols = columns(h)
        lc = twice(last_g[h])
        state = cback[state_rows(h), :]
        lv_out[1, :, cols] = (fin[0, :, cols] + lc * dot_nt(guest_kv[1, :, cols], state)).astype(BF16)
        lv_out[2, :, cols] = (fin[1, :, cols] + lc * dot_nn(guest_kv[0, :, cols], state)).astype(BF16)
        return 0

    lax.fori_loop(0, heads, finish_block, 0)
    lv_copies += to_partners(lv_out.at[1:3], lambda level: lv_in.at[level, 1:3], lv_ss, lv_rs, levels)

    def finish(h, _):
        cols = columns(h)
        lc = twice(colb[2 * heads + h])
        state = cback[state_rows(h), :]
        k = pk[:, cols]
        dk = dkin[:, cols] + lc * dot_nt(pv[:, cols], state)
        dv = ret[:, cols] + lc * dot_nn(k, state)
        pk[:, cols] = dk.astype(BF16)
        pv[:, cols] = dv.astype(BF16)
        return 0

    lax.fori_loop(0, heads, finish, 0)
    for copy in p2 + b1 + b2 + h_copies + mid + back_mid:
        copy.wait_send()
    for copy in lv_copies:
        copy.wait()
    for i in range(3):
        guest_out[i] = guest_of(lv_out[i], lambda level: lv_in[level, i])


def place_kernel(slots, guest, dq, dk, dv, oq, ok, ov, sem):
    slot = slots[lax.axis_index("dp")]
    per = 4
    chunk = per * BLOCK_LEN

    def one(c, _):
        inside = slot // per == c
        at = pl.multiple_of(c * chunk, chunk)
        for i, (src, dst) in enumerate(((dq, oq), (dk, ok), (dv, ov))):

            @pl.when(jnp.logical_not(inside))
            def _():
                rows = pl.ds(at, chunk)
                pltpu.make_async_copy(src.at[rows], dst.at[rows], sem.at[i]).start()

            @pl.when(inside)
            def _():
                for b in range(per):
                    rows = pl.ds(pl.multiple_of(at + b * BLOCK_LEN, BLOCK_LEN), BLOCK_LEN)

                    @pl.when(c * per + b == slot)
                    def _():
                        pltpu.make_async_copy(guest.at[i], dst.at[rows], sem.at[i]).start()

                    @pl.when(c * per + b != slot)
                    def _():
                        pltpu.make_async_copy(src.at[rows], dst.at[rows], sem.at[i]).start()

        return 0

    lax.fori_loop(0, dq.shape[0] // chunk, one, 0)
    for i, (src, dst) in enumerate(((dq, oq), (dk, ok), (dv, ov))):
        pltpu.make_async_copy(src, dst, sem.at[i]).wait()


def local(count, hcount, queries, keys, values, out_grad, norm_gain, table, index, lengths, partners, slots):
    tokens, width = queries.shape
    heads = table.shape[0]
    tiles = tokens // TILE
    levels = count.bit_length() - 1
    group = count // 2
    span = heads * HEAD_DIM // group
    smem = pl.BlockSpec(memory_space=pltpu.SMEM)
    vmem = pl.BlockSpec(memory_space=pltpu.VMEM)
    any_ = pl.BlockSpec(memory_space=pl.ANY)
    full = jax.ShapeDtypeStruct((tokens, width), BF16)
    V = pltpu.VMEM
    D = pltpu.SemaphoreType.DMA
    held = V((tokens, width), BF16)
    state = V((heads * HEAD_DIM, HEAD_DIM), BF16)
    part = V((group, span, HEAD_DIM), BF16)
    dq, dk, dv, guest = pl.pallas_call(
        functools.partial(main_kernel, count, hcount, heads, tokens),
        out_shape=(held, held, held, V((3, BLOCK_LEN, width), BF16)),
        in_specs=[smem, smem, smem, vmem, vmem, vmem, any_, any_, any_, any_],
        out_specs=(vmem, vmem, vmem, vmem),
        scratch_shapes=[
            held,
            V((heads, tokens, tokens), BF16),
            V((heads, TILE, tiles * (tiles + 1) // 2 * TILE), F32),
            V((tokens, tokens), BF16),
            V((tokens, width), F32), V((tokens, width), F32), V((tokens, width), BF16),
            V((3 * heads, tokens, 128), F32), V((tokens, 128), F32), V((8, tokens), F32),
            V((tokens, 128), BF16), V((tokens, 128), BF16),
            V((2, BLOCK_LEN, width), BF16), V((heads, BLOCK_LEN, 128), F32), V((2, BLOCK_LEN, width), F32),
            V((heads * HEAD_DIM, HEAD_DIM), F32),
            V((8, tokens), F32), V((levels, 8, tokens), F32),
            V((4, BLOCK_LEN, width), BF16), V((levels, 4, BLOCK_LEN, width), BF16),
            V((count, 8, 128), F32), V((8, 128), F32),
            state, part, part, state, part, part, state,
            V((4, span // 2, HEAD_DIM), BF16), V((4, span // 2, HEAD_DIM), BF16),
            V((2, 8, tokens // 2), F32), V((2, hcount, 8, tokens // 2), F32),
            V((3, BLOCK_LEN, width), BF16), V((levels, 3, BLOCK_LEN, width), BF16),
            D((4,)), D((levels,)), D((levels,)), D((3 * levels,)), D((3 * levels,)),
            D((count,)), D((count,)), D((2 * group,)), D((2 * group,)), D((2 * group,)), D((2 * group,)),
            D((2 * group,)), D((2 * group,)), D((2 * group,)), D((2 * group,)), D((4,)), D((4,)),
            D((2 * hcount,)), D((2 * hcount,)), D((2 * levels,)), D((2 * levels,)),
        ],
        compiler_params=pltpu.CompilerParams(
            collective_id=0, has_side_effects=True, vmem_limit_bytes=50 * 1024 * 1024
        ),
    )(lengths, partners, slots, table, index, norm_gain.reshape(1, width), queries, keys, values, out_grad)

    kept = [pltpu.with_memory_space_constraint(a, pltpu.VMEM) for a in (guest, dq, dk, dv)]
    return pl.pallas_call(
        place_kernel,
        out_shape=(full, full, full),
        in_specs=[smem, vmem, vmem, vmem, vmem],
        out_specs=(any_, any_, any_),
        scratch_shapes=[D((3,))],
        compiler_params=pltpu.CompilerParams(vmem_limit_bytes=1024 * 1024),
    )(slots, *kept)


def solution(mesh):
    placed = (
        P("dp", "head"), P("dp", "head"), P("dp", "head"), P("dp", "head"),
        P("head"), P("head", None), P("head", "dp"), P(), P(), P(),
    )
    return jax.shard_map(
        functools.partial(local, mesh.shape["dp"], mesh.shape["head"]),
        mesh=mesh,
        in_specs=placed,
        out_specs=(P("dp", "head"), P("dp", "head"), P("dp", "head")),
        check_vma=False,
    )
```
